32 devices in a mesh: grp: 4 (over y, x), dev: 8 (over z, core).
Axes of the slice: x: 2, y: 2, z: 4, core: 2. Of those that a mesh axis runs over, the one named last changes fastest.
Arguments:
- locations: float32 [32, 3, 256], P(('grp', 'dev')), may hold values from 0 to 1
- neighbours: int32 [32, 4], P(('grp', 'dev')), may hold values from -1 to 30, as said below
- observations: float32 [32, 8, 256], P(('grp', 'dev')), may hold values from -63 to 63
- noise_prec: float32 [32, 8, 256], P(('grp', 'dev')), may hold values from 0.5 to 4
Outputs:
- solution: float32 [32, 8, 256], P(('grp', 'dev'))
- residual: float32 [32, 8, 256], P(('grp', 'dev'))
The draws below stay inside these ranges and needn't reach their ends.
Inputs may be any that keep to these rules, and one draw needn't show every extreme that they name: `neighbours`: row b holds b - 1 in slot 0 (-1 for block 0); in slot 1 a block drawn from the range from max(b - 1, 0) * 1 to b - 2, or -1 where that range is empty; in slots 2 and 3 two different blocks below min(8, max(b - 1, 0)), -1 in a slot where fewer exist. All listed blocks of a row differ.
All inputs are finite; a program needn't handle non-finite values.
Results may differ from the reference program's by a relative error of at most 0.0003.
Values sent between devices are 32-bit elements; how exact they have to be, the bound alone decides.
No kernel may reach another device: no remote copies, remote signals or barrier semaphores. Data moves between devices by JAX's collectives and lax.ppermute only.
A program may use at most 128 MiB of HBM per device.

```python
import math
import jax
import jax.numpy as jnp
from jax import lax

BS = 256
NEIGH = 4
BLK_DEV = 1
NV = 8
ITERS = 2
NBLK = 32
NCOARSE = 8


def draw_neighbours(key, part):
    block_index = jnp.arange(NBLK, dtype=jnp.int32)
    device_index = block_index // BLK_DEV
    window_first = jnp.maximum(device_index - 1, 0) * BLK_DEV
    window_size = jnp.maximum(block_index - 1 - window_first, 0)
    subkeys = jax.random.split(jax.random.fold_in(key, 11), 3)
    near_pick = window_first + jax.random.randint(subkeys[0], (NBLK,), 0, jnp.maximum(window_size, 1))
    near_pick = jnp.where(window_size > 0, near_pick, -1)
    coarse_limit = jnp.minimum(NCOARSE, window_first)
    first_top = coarse_limit - 2
    first_draw = jax.random.randint(subkeys[1], (NBLK,), 0, jnp.maximum(first_top + 1, 1))
    coarse_one = jnp.where(first_top >= 0, first_draw, -1)
    second_top = coarse_limit - 1
    second_draw = jax.random.randint(subkeys[2], (NBLK,), 0, jnp.maximum(second_top + 1, 1))
    second_draw = jnp.where(second_draw == coarse_one, second_top, second_draw)
    coarse_two = jnp.where(second_top >= 0, second_draw, -1)
    return jnp.stack([block_index - 1, near_pick, coarse_one, coarse_two], axis=1).astype(jnp.int32)


def draw_observations(key, part):
    subkeys = jax.random.split(jax.random.fold_in(key, 23), 2)
    values = jnp.clip(jax.random.normal(subkeys[0], (NBLK, NV, BS), jnp.float32), -4.0, 4.0)
    rising = 1.0 + 2.0 * jnp.arange(NBLK, dtype=jnp.float32) / (NBLK - 1)
    field_scale = jnp.exp(jax.random.uniform(subkeys[1], (NV,), jnp.float32, math.log(0.3), math.log(3.0)))
    return values * rising[:, None, None] * field_scale[None, :, None]


def block_scale(stream_key, shape, pieces, least, top_value):
    gain, own = 1.0, jax.random.fold_in(stream_key, 6)
    for axis_at, shards_of in pieces:
        heights = jnp.exp(jax.random.uniform(jax.random.fold_in(own, axis_at), (shards_of,), jnp.float32, least / len(pieces), top_value / len(pieces)))
        gain = gain * jnp.repeat(heights, shape[axis_at] // shards_of).reshape([-1 if axis == axis_at else 1 for axis in range(len(shape))])
    return gain


def setup_inputs(seed: int = 0) -> dict:
    key_of = jax.random.split(jax.random.key(seed), 5)
    locations = jnp.clip(1.0 * jax.random.uniform(key_of[0], (NBLK, 3, BS), jnp.float32) ** block_scale(key_of[0], (NBLK, 3, BS), ((0, 32),), -0.2, 0.2), 0.0, 1.0)
    neighbours = draw_neighbours(jax.random.fold_in(key_of[4], 71), 0)
    observations = draw_observations(jax.random.fold_in(key_of[4], 71), 0)
    noise_prec = jnp.clip(jnp.exp(math.log(4.0) - 2.0794415 * jax.random.uniform(key_of[3], (NBLK, NV, BS), jnp.float32) ** block_scale(key_of[3], (NBLK, NV, BS), ((0, 32),), -0.2, 0.2)), 0.5, 4.0)
    return dict(locations=locations, neighbours=neighbours, observations=observations, noise_prec=noise_prec)


SCALE_LENGTH = 0.5
NUGGET = 0.5
SQRT_THREE = math.sqrt(3.0)
HIGHEST = lax.Precision.HIGHEST

def kernel_factor(point_set, point_mask, own_size):
    offsets = point_set[:, :, None] - point_set[:, None, :]
    distance = jnp.sqrt(lax.optimization_barrier(jnp.sum(offsets * offsets, axis=0)))
    scaled = SQRT_THREE / SCALE_LENGTH * distance
    covariance = (1.0 + scaled) * jnp.exp(-scaled)
    order_size = point_set.shape[1]
    identity = jnp.eye(order_size, dtype=point_set.dtype)
    diagonal_term = NUGGET * point_mask + (1.0 - point_mask)
    covariance = covariance * (point_mask[:, None] * point_mask[None, :]) + identity * diagonal_term[:, None]
    factor_lower = jnp.linalg.cholesky(covariance)
    unit_tail = identity[:, order_size - own_size:]
    return lax.linalg.triangular_solve(factor_lower, unit_tail, left_side=True, lower=True, transpose_a=True)

def reference(locations, neighbours, observations, noise_prec):
    block_ids = neighbours.astype(jnp.int32)
    slot_live = (block_ids >= 0).astype(locations.dtype)
    safe_ids = jnp.maximum(block_ids, 0).astype(jnp.int32)

    def gather_slots(field):
        picked = field[safe_ids] * slot_live[:, :, None, None]
        picked = jnp.transpose(picked, (0, 2, 1, 3)).reshape(NBLK, field.shape[1], NEIGH * BS)
        return jnp.concatenate([picked, field], axis=2)
    point_sets = gather_slots(locations)
    point_mask = jnp.concatenate([jnp.repeat(slot_live, BS, axis=1), jnp.ones((NBLK, BS), locations.dtype)], axis=1)
    factors = lax.map(lambda pair: kernel_factor(pair[0], pair[1], BS), (point_sets, point_mask))

    def apply_transpose(field):
        return jnp.einsum('bvk,bkp->bvp', gather_slots(field), factors, precision=HIGHEST)

    def apply_factor(field):
        spread = jnp.einsum('bvp,bkp->bvk', field, factors, precision=HIGHEST)
        own_part = spread[:, :, NEIGH * BS:]
        slot_parts = spread[:, :, :NEIGH * BS].reshape(NBLK, NV, NEIGH, BS) * slot_live[:, None, :, None]
        slot_parts = jnp.transpose(slot_parts, (0, 2, 1, 3)).reshape(NBLK * NEIGH, NV, BS)
        return own_part + jnp.zeros_like(own_part).at[safe_ids.reshape(-1)].add(slot_parts)

    def operator(field):
        return apply_factor(apply_transpose(field)) + noise_prec * field
    solution = jnp.zeros_like(observations)
    residual = observations
    direction = observations
    norm_now = lax.optimization_barrier(jnp.sum(residual * residual, axis=(0, 2)))
    for iteration in range(ITERS):
        image = operator(direction)
        alpha = norm_now / lax.optimization_barrier(jnp.sum(direction * image, axis=(0, 2)))
        solution = solution + alpha[None, :, None] * direction
        residual = residual - alpha[None, :, None] * image
        if iteration + 1 < ITERS:
            norm_next = lax.optimization_barrier(jnp.sum(residual * residual, axis=(0, 2)))
            direction = residual + (norm_next / norm_now)[None, :, None] * direction
            norm_now = norm_next
    return (solution, residual)
```

```python
import functools
import math

import jax
import jax.numpy as jnp
from jax import lax
from jax.experimental import pallas as pl
from jax.experimental.pallas import tpu as pltpu
from jax.sharding import PartitionSpec as P

SCALE_LENGTH = 0.5
NUGGET = 0.5
SQRT_THREE = math.sqrt(3.0)
LANES = 128
HIGHEST = lax.Precision.HIGHEST
F32 = jnp.float32
NN = (((1,), (0,)), ((), ()))
NT = (((1,), (1,)), ((), ()))
AXES = ("grp", "dev")
VMEM_LIMIT = 48 * 1024 * 1024


def split(value):
    high = value.astype(jnp.bfloat16)
    return high, (value - high.astype(F32)).astype(jnp.bfloat16)


def dot(left, right, dims=NN, precision=None):
    return lax.dot_general(left, right, dims, precision=precision, preferred_element_type=F32)


def dot_three(left, right, dims=NN):
    return dot(left[0], right[0], dims) + (dot(left[0], right[1], dims) + dot(left[1], right[0], dims))


def inverse(matrix, beside=()):
    order = matrix.shape[0]
    rows = lax.broadcasted_iota(jnp.int32, (order, order), 0)
    columns = lax.broadcasted_iota(jnp.int32, (order, order), 1)
    identity = (rows == columns).astype(F32)
    start = 2.0 / (2.0 * NUGGET + order)
    least = start * NUGGET
    ahead = start * matrix
    guess = None
    beside = list(beside)
    while True:
        reached = least * (2.0 - least)
        centre = 2.0 / (1.0 + reached)
        least = centre * reached
        ahead_parts = split(ahead)
        if guess is None:
            guess = (centre * start) * (2.0 * identity - ahead)
        else:
            guess = centre * (2.0 * guess - dot_three(split(guess), ahead_parts))
        if beside:
            beside.pop(0)()
        if 1.0 - least < 1e-3:
            break
        ahead = centre * (2.0 * ahead - dot_three(ahead_parts, ahead_parts))
    for work in beside:
        work()
    error = identity - dot(matrix, guess, precision=HIGHEST)
    return guess + dot_three(split(guess), split(error))


def table_fields(entry, fields):
    return jnp.concatenate([entry[at : at + fields] for at in range(0, entry.shape[0] - 8, fields)], axis=1)


def table_places(entry, fields, pieces):
    first = fields * pieces
    return jnp.concatenate([entry[first + 4 * at : first + 4 * at + 4] for at in range(pieces)], axis=1)


def slot_list(slots):
    return [slot for slot in range(slots) if slot != 1]


def factor_kernel(sizes, nbr, me, table, noise, part, near_own, near_prev, back_out, last_out, blocks):
    fields, points, coarse, slots = sizes
    pieces = points // LANES
    used = slot_list(slots)
    count = len(used) + 1
    ids = [nbr[0, slot] for slot in used] + [me[0]]
    entries = [table[jnp.maximum(index, 0)] for index in ids]
    live = [(index >= 0).astype(F32) for index in ids]
    values = [table_fields(entry, fields) * alive for entry, alive in zip(entries, live)]
    places = [table_places(entry, fields, pieces) * (SQRT_THREE / SCALE_LENGTH) for entry in entries]
    turned = [jnp.transpose(jnp.concatenate([place, place], axis=0)) for place in places]
    rows_at_once = 64

    def build(i, j):
        across = places[j]
        alive = live[i] * live[j]
        for first in range(0, points, rows_at_once):
            down = turned[i][first : first + rows_at_once]
            total = None
            for k in range(3):
                offset = down[:, k : k + 1] - across[k : k + 1, :]
                total = offset * offset if total is None else total + offset * offset
            scaled = jnp.sqrt(total)
            value = (1.0 + scaled) * jnp.exp(-scaled) * alive
            if i == j:
                row = lax.broadcasted_iota(jnp.int32, value.shape, 0) + first
                column = lax.broadcasted_iota(jnp.int32, value.shape, 1)
                value = value + jnp.where(row == column, NUGGET * live[i] + (1.0 - live[i]), 0.0)
            blocks[i, j, first : first + rows_at_once, :] = value

    pairs = [(i, j) for i in range(count) for j in range(i + 1)]
    build(0, 0)
    later = [functools.partial(build, i, j) for i, j in pairs if (i, j) != (0, 0)]
    lower = {}
    last = None
    for k in range(count):
        middle = inverse(blocks[k, k], later if k == 0 else ())
        if k == count - 1:
            last = middle
            break
        side = {i: blocks[i, k] for i in range(k + 1, count)}
        for i in range(k + 1, count):
            lower[i, k] = dot(side[i], middle, precision=HIGHEST)
        side_parts = {i: split(side[i]) for i in side}
        for i in range(k + 1, count):
            left = split(lower[i, k])
            for j in range(k + 1, i + 1):
                blocks[i, j] = blocks[i, j] - dot_three(left, side_parts[j], NT)
    own = count - 1
    back = {}
    for k in range(own - 1, -1, -1):
        total = lower[own, k]
        for j in range(k + 1, own):
            total = total - dot_three(split(back[j]), split(lower[j, k]))
        back[k] = total
    for k in range(own):
        back_out[:, k * points : (k + 1) * points] = back[k]
    last_out[...] = last

    middle, spread, slot_parts = apply_block(values, back_out, last_out[...], points)
    own_part = spread + noise[0] * values[own]
    near_own[...] = own_part
    near_prev[...] = slot_parts[0]
    part[...] = jnp.zeros_like(part)
    part[coarse] = middle * spread + noise[0] * values[own] * values[own]
    add_coarse(part, coarse, ids, slot_parts, own_part)


def apply_block(values, back, last, points):
    own = len(values) - 1
    middle = values[own]
    for k in range(own):
        middle = middle - dot_three(split(values[k]), split(back[:, k * points : (k + 1) * points]), NT)
    spread = dot_three(split(middle), split(last))
    spread_parts = split(spread)
    slot_parts = [-dot_three(spread_parts, split(back[:, k * points : (k + 1) * points])) for k in range(own)]
    return middle, spread, slot_parts


def add_coarse(part, coarse, ids, slot_parts, own_part):
    for index, value in zip(ids, slot_parts + [own_part]):

        @pl.when((index >= 0) & (index < coarse))
        def _(index=index, value=value):
            part[index] = part[index] + value


def step_kernel(
    sizes, nbr, me, table, noise, summed, near_image, prev_image, back, last, sends, image_out, residual_out, ratio_out
):
    fields, points, coarse, slots = sizes
    pieces = points // LANES
    devices = table.shape[0]
    used = slot_list(slots)
    ids = [nbr[0, slot] for slot in used] + [me[0]]
    square = jnp.zeros((fields, points), F32)
    for block in range(devices):
        value = table_fields(table[block], fields)
        square = square + value * value
    norm_now = jnp.sum(square, axis=1, keepdims=True)
    product = jnp.sum(summed[coarse], axis=1, keepdims=True)
    alpha = norm_now / product
    observed, images = [], []
    for at, index in enumerate(ids):
        alive = (index >= 0).astype(F32)
        observed.append(table_fields(table[jnp.maximum(index, 0)], fields) * alive)
        image = summed[jnp.clip(index, 0, coarse - 1)]
        if at == len(ids) - 1:
            image = jnp.where(index < coarse, image, near_image[...])
        elif at == 0:
            image = jnp.where(index < coarse, image, prev_image[...])
        images.append(image * alive)
    values = [value - alpha * image for value, image in zip(observed, images)]
    middle, spread, slot_parts = apply_block(values, back, last[...], points)
    residual, image = values[-1], images[-1]
    own_part = spread + noise[0] * residual
    inner = jnp.sum(middle * spread + noise[0] * residual * residual, axis=1, keepdims=True)
    cross = jnp.sum(residual * image, axis=1, keepdims=True)
    square = jnp.sum(residual * residual, axis=1, keepdims=True)
    lane = lax.broadcasted_iota(jnp.int32, (fields, LANES), 1)
    scalars = jnp.where(lane == 0, inner, jnp.where(lane == 1, cross, jnp.where(lane == 2, square, 0.0)))
    clear = jnp.zeros((fields * pieces, LANES), F32)
    for block in range(devices):
        sends[block] = jnp.concatenate([clear, scalars], axis=0)
    for index, value in zip(ids, slot_parts + [own_part]):

        @pl.when(index >= 0)
        def _(index=index, value=value):
            for piece in range(pieces):
                sends[index, piece * fields : (piece + 1) * fields, :] = value[:, piece * LANES : (piece + 1) * LANES]

    image_out[...] = image
    residual_out[...] = residual
    ratio_out[...] = jnp.where(lane == 0, alpha, jnp.where(lane == 1, norm_now, product))


def finish_kernel(sizes, received, image, residual, ratios, observed, solution_out, residual_out):
    fields, points, coarse, slots = sizes
    pieces = points // LANES
    total = received[0]
    for block in range(1, received.shape[0]):
        total = total + received[block]
    spread = jnp.concatenate([total[at * fields : (at + 1) * fields] for at in range(pieces)], axis=1)
    scalars = total[pieces * fields :]
    alpha, norm_first, product_first = ratios[:, 0:1], ratios[:, 1:2], ratios[:, 2:3]
    inner, cross, norm_now = scalars[:, 0:1], scalars[:, 1:2], scalars[:, 2:3]
    beta = norm_now / norm_first
    product = inner + beta * (2.0 * cross + beta * product_first)
    step = norm_now / product
    direction = residual[...] + beta * observed[0]
    solution_out[0] = alpha * observed[0] + step * direction
    residual_out[0] = residual[...] - step * (spread + beta * image[...])


def call(kernel, sizes, outs, in_spaces, scratch=(), flops=0):
    return pl.pallas_call(
        functools.partial(kernel, sizes),
        out_shape=[jax.ShapeDtypeStruct(shape, F32) for shape in outs],
        in_specs=[pl.BlockSpec(memory_space=space) for space in in_spaces],
        out_specs=[pl.BlockSpec(memory_space=pltpu.VMEM)] * len(outs),
        scratch_shapes=list(scratch),
        compiler_params=pltpu.CompilerParams(vmem_limit_bytes=VMEM_LIMIT),
    )


def summed_over(value, axis):
    size = lax.axis_size(axis)
    if size & (size - 1):
        return lax.psum(value, axis)
    reach = 1
    while reach < size:
        value = value + lax.ppermute(value, axis, [(at, at ^ reach) for at in range(size)])
        reach *= 2
    return value


def local(locations, neighbours, observations, noise_prec):
    blocks, _, points = locations.shape
    fields = observations.shape[1]
    slots = neighbours.shape[1]
    assert blocks == 1
    pieces = points // LANES
    coarse = lax.axis_size("dev")
    devices = coarse * lax.axis_size("grp")
    sizes = (fields, points, coarse, slots)
    depth = (len(slot_list(slots))) * points
    me = lax.axis_index(AXES).astype(jnp.int32).reshape(1)
    smem, vmem = pltpu.SMEM, pltpu.VMEM

    def cut(rows):
        return rows.reshape(rows.shape[0], pieces, LANES).transpose(1, 0, 2).reshape(-1, LANES)

    packed = jnp.concatenate([cut(observations[0]), cut(jnp.pad(locations[0], ((0, 1), (0, 0))))], axis=0)
    table = lax.all_to_all(jnp.broadcast_to(packed, (devices,) + packed.shape), AXES, 0, 0, tiled=True)
    part, near_own, near_prev, back, last = call(
        factor_kernel,
        sizes,
        [(coarse + 1, fields, points), (fields, points), (fields, points), (points, depth), (points, points)],
        [smem, smem, vmem, vmem],
        [pltpu.VMEM((slots, slots, points, points), F32)],
    )(neighbours, me, table, noise_prec)
    near_image = near_own + lax.ppermute(near_prev, AXES, [(at, at - 1) for at in range(1, devices)])
    prev_image = lax.ppermute(near_image, AXES, [(at, at + 1) for at in range(devices - 1)])
    summed = summed_over(summed_over(part, "dev"), "grp")
    sends, image, residual, ratios = call(
        step_kernel,
        sizes,
        [(devices, 3 * fields, LANES), (fields, points), (fields, points), (fields, LANES)],
        [smem, smem] + [vmem] * 7,
    )(neighbours, me, table, noise_prec, summed, near_image, prev_image, back, last)
    received = lax.all_to_all(sends, AXES, 0, 0, tiled=True)
    return tuple(
        call(finish_kernel, sizes, [observations.shape] * 2, [vmem] * 5)(
            received, image, residual, ratios, observations
        )
    )


def solution(mesh):
    placed = (
        P(AXES, None, None),
        P(AXES, None),
        P(AXES, None, None),
        P(AXES, None, None),
    )
    return jax.shard_map(
        local,
        mesh=mesh,
        in_specs=placed,
        out_specs=(P(AXES, None, None), P(AXES, None, None)),
        check_vma=False,
    )
```

```python
import functools
import math

import jax
import jax.numpy as jnp
from jax import lax
from jax.experimental import pallas as pl
from jax.experimental.pallas import tpu as pltpu
from jax.sharding import PartitionSpec as P

SCALE_LENGTH = 0.5
NUGGET = 0.5
SQRT_THREE = math.sqrt(3.0)
LANES = 128
HIGHEST = lax.Precision.HIGHEST
F32 = jnp.float32
NN = (((1,), (0,)), ((), ()))
NT = (((1,), (1,)), ((), ()))
AXES = ("grp", "dev")
VMEM_LIMIT = 48 * 1024 * 1024


def split(value):
    high = value.astype(jnp.bfloat16)
    return high, (value - high.astype(F32)).astype(jnp.bfloat16)


def dot(left, right, dims=NN, precision=None):
    return lax.dot_general(left, right, dims, precision=precision, preferred_element_type=F32)


def dot_three(left, right, dims=NN):
    return dot(left[0], right[0], dims) + (dot(left[0], right[1], dims) + dot(left[1], right[0], dims))


def inverse(matrix, beside=()):
    order = matrix.shape[0]
    rows = lax.broadcasted_iota(jnp.int32, (order, order), 0)
    columns = lax.broadcasted_iota(jnp.int32, (order, order), 1)
    identity = (rows == columns).astype(F32)
    start = 2.0 / (2.0 * NUGGET + order)
    least = start * NUGGET
    ahead = start * matrix
    guess = None
    beside = list(beside)
    while True:
        reached = least * (2.0 - least)
        centre = 2.0 / (1.0 + reached)
        least = centre * reached
        ahead_parts = split(ahead)
        if guess is None:
            guess = (centre * start) * (2.0 * identity - ahead)
        else:
            guess = centre * (2.0 * guess - dot_three(split(guess), ahead_parts))
        if beside:
            beside.pop(0)()
        if 1.0 - least < 1e-3:
            break
        ahead = centre * (2.0 * ahead - dot_three(ahead_parts, ahead_parts))
    for work in beside:
        work()
    error = identity - dot(matrix, guess, precision=HIGHEST)
    return guess + dot_three(split(guess), split(error))


def slot_list(slots):
    return [slot for slot in range(slots) if slot != 1]


def mirrored(index, size):
    bits = size.bit_length() - 1
    return sum(((index >> bit) & 1) << (bits - 1 - bit) for bit in range(bits))


def covariance(first, second, alive, same):
    points = second.shape[1]
    rows_at_once = 64
    parts = []
    for start in range(0, points, rows_at_once):
        down = first[start : start + rows_at_once]
        total = None
        for k in range(3):
            offset = down[:, k : k + 1] - second[k : k + 1, :]
            total = offset * offset if total is None else total + offset * offset
        scaled = jnp.sqrt(total)
        value = (1.0 + scaled) * jnp.exp(-scaled) * alive
        if same:
            row = lax.broadcasted_iota(jnp.int32, value.shape, 0) + start
            column = lax.broadcasted_iota(jnp.int32, value.shape, 1)
            value = value + jnp.where(row == column, NUGGET * alive + (1.0 - alive), 0.0)
        parts.append(value)
    return jnp.concatenate(parts, axis=0)


def scaled_places(entry, fields):
    return entry[fields:] * (SQRT_THREE / SCALE_LENGTH)


def live_of(index):
    return (index >= 0).astype(F32)


def pack_kernel(sizes, locations, observed, packed):
    fields = sizes[0]
    packed[...] = jnp.zeros_like(packed)
    packed[:fields] = observed[0]
    packed[fields : fields + 3] = locations[0]


def near_kernel(sizes, nbr, before, mine, middle_out, lower_out, left_out):
    fields = sizes[0]
    alive = live_of(nbr[0, 0])
    places = [scaled_places(before[...], fields), scaled_places(mine[...], fields)]
    turned = [jnp.transpose(place) for place in places]
    side, own = [], []
    first = covariance(turned[0], places[0], alive, True)
    middle = inverse(
        first,
        [
            lambda: side.append(covariance(turned[1], places[0], alive, False)),
            lambda: own.append(covariance(turned[1], places[1], 1.0, True)),
        ],
    )
    lower = dot(side[0], middle, precision=HIGHEST)
    middle_out[...] = middle
    lower_out[...] = lower
    left_out[...] = own[0] - dot_three(split(lower), split(side[0]), NT)


def factor_kernel(
    sizes, nbr, me, before, mine, table, noise, middle_in, lower_in, left_in, part, near_own, near_prev, back_out, last_out, blocks
):
    fields, points, coarse, slots = sizes
    used = slot_list(slots)
    own = len(used)
    ids = [nbr[0, slot] for slot in used] + [me[0]]
    here = lax.rem(me[0], coarse)
    entries = [before[...]]
    entries += [table[mirrored(jnp.maximum(index, 0) ^ here, coarse)] for index in ids[1:own]]
    entries += [mine[...]]
    live = [live_of(index) for index in ids]
    values = [entry[:fields] * alive for entry, alive in zip(entries, live)]
    places = [scaled_places(entry, fields) for entry in entries]
    turned = [jnp.transpose(place) for place in places]

    def build(i, j):
        blocks[i, j] = covariance(turned[i], places[j], live[i] * live[j], i == j)

    halves, lower = {}, {(own, 0): lower_in[...]}

    def parts_of(i, j):
        if (i, j) not in halves:
            halves[i, j] = split(blocks[i, j])
        return halves[i, j]

    def multiply(i, k, middle):
        lower[i, k] = dot(blocks[i, k], middle, precision=HIGHEST)

    def update(i, j, k):
        blocks[i, j] = blocks[i, j] - dot_three(split(lower[i, k]), parts_of(j, k), NT)

    def open_column(i):
        build(i, 0)
        multiply(i, 0, middle_in[...])

    def leave(i, j):
        build(i, j)
        update(i, j, 0)

    blocks[own, own] = left_in[...]
    open_column(1)
    leave(1, 1)
    later = []
    for i in range(2, own):
        later.append(functools.partial(open_column, i))
        later += [functools.partial(leave, i, j) for j in range(1, i + 1)]
    later += [functools.partial(leave, own, j) for j in range(1, own)]
    back = {}

    def go_back(k):
        total = lower[own, k]
        for j in range(k + 1, own):
            total = total - dot_three(split(back[j]), split(lower[j, k]))
        back[k] = total

    for k in range(1, own):
        middle = inverse(blocks[k, k], later)
        for i in range(k + 1, own + 1):
            multiply(i, k, middle)
        update(k + 1, k + 1, k)
        later = [
            functools.partial(update, i, j, k)
            for i in range(k + 1, own + 1)
            for j in range(k + 1, i + 1)
            if (i, j) != (k + 1, k + 1)
        ]
    last = inverse(blocks[own, own], [functools.partial(go_back, k) for k in range(own - 1, -1, -1)])
    for k in range(own):
        back_out[:, k * points : (k + 1) * points] = back[k]
    last_out[...] = last

    middle, spread, slot_parts = apply_block(values, back, last)
    own_part = spread + noise[0] * values[own]
    near_own[...] = own_part
    near_prev[...] = slot_parts[0]
    part[...] = jnp.zeros_like(part)
    product = jnp.sum(middle * spread + noise[0] * values[own] * values[own], axis=1, keepdims=True)
    square = jnp.sum(values[own] * values[own], axis=1, keepdims=True)
    part[coarse] = in_lanes([product, square], (fields, points))
    for index, value in zip(ids, slot_parts + [own_part]):

        @pl.when((index >= 0) & (index < coarse))
        def _(index=index, value=value):
            part[index] = part[index] + value


def in_lanes(columns, shape):
    lane = lax.broadcasted_iota(jnp.int32, shape, 1)
    total = jnp.zeros(shape, F32)
    for at, column in enumerate(columns):
        total = jnp.where(lane == at, column, total)
    return total


def apply_block(values, back, last):
    own = len(values) - 1
    middle = values[own]
    for k in range(own):
        middle = middle - dot_three(split(values[k]), split(back[k]), NT)
    spread = dot_three(split(middle), split(last))
    spread_parts = split(spread)
    slot_parts = [-dot_three(spread_parts, split(back[k])) for k in range(own)]
    return middle, spread, slot_parts


def step_kernel(
    sizes, nbr, me, before, mine, table, noise, summed, near_own, near_prev, own_before, from_after, back, last,
    sends, near_out, own_out, image_out, residual_out, ratio_out,
):
    fields, points, coarse, slots = sizes
    used = slot_list(slots)
    own = len(used)
    ids = [nbr[0, slot] for slot in used] + [me[0]]
    here = lax.rem(me[0], coarse)
    product = summed[coarse][:, 0:1]
    norm_now = summed[coarse][:, 1:2]
    alpha = norm_now / product
    values = []
    for at, index in enumerate(ids):
        image = summed[jnp.clip(index, 0, coarse - 1)]
        if at == 0:
            observed = before[:fields]
            image = jnp.where(index < coarse, image, own_before[...] + near_prev[...])
        elif at == own:
            observed = mine[:fields]
            image = jnp.where(index < coarse, image, near_own[...] + from_after[...])
        else:
            observed = table[mirrored(jnp.maximum(index, 0) ^ here, coarse)][:fields]
        values.append((observed - alpha * image) * live_of(index))
    back_parts = {k: back[:, k * points : (k + 1) * points] for k in range(own)}
    middle, spread, slot_parts = apply_block(values, back_parts, last[...])
    residual = values[own]
    own_part = spread + noise[0] * residual
    inner = jnp.sum(middle * spread + noise[0] * residual * residual, axis=1, keepdims=True)
    cross = jnp.sum(residual * image, axis=1, keepdims=True)
    square = jnp.sum(residual * residual, axis=1, keepdims=True)
    sends[...] = jnp.zeros_like(sends)
    sends[coarse] = in_lanes([inner, cross, square], (fields, points))
    for index, value in zip(ids[1:own], slot_parts[1:]):

        @pl.when(index >= 0)
        def _(index=index, value=value):
            place = mirrored(index ^ here, coarse)
            sends[place] = sends[place] + value

    near_out[...] = slot_parts[0]
    own_out[...] = own_part
    image_out[...] = image
    residual_out[...] = residual
    ratio_out[...] = in_lanes([alpha, norm_now, product], (fields, LANES))


def finish_kernel(
    sizes, me, received, own_part, from_after, image, residual, ratios, observed, solution_out, residual_out
):
    coarse = sizes[2]
    owner = (me[0] < coarse).astype(F32)
    spread = own_part[...] + from_after[...] + owner * received[0]
    scalars = received[1]
    alpha, norm_first, product_first = ratios[:, 0:1], ratios[:, 1:2], ratios[:, 2:3]
    inner, cross, norm_now = scalars[:, 0:1], scalars[:, 1:2], scalars[:, 2:3]
    beta = norm_now / norm_first
    product = inner + beta * (2.0 * cross + beta * product_first)
    step = norm_now / product
    direction = residual[...] + beta * observed[0]
    solution_out[0] = alpha * observed[0] + step * direction
    residual_out[0] = residual[...] - step * (spread + beta * image[...])


def call(kernel, sizes, outs, in_spaces, scratch=()):
    return pl.pallas_call(
        functools.partial(kernel, sizes),
        out_shape=[jax.ShapeDtypeStruct(shape, F32) for shape in outs],
        in_specs=[pl.BlockSpec(memory_space=space) for space in in_spaces],
        out_specs=[pl.BlockSpec(memory_space=pltpu.VMEM)] * len(outs),
        scratch_shapes=list(scratch),
        compiler_params=pltpu.CompilerParams(vmem_limit_bytes=VMEM_LIMIT),
    )


def powers(size):
    assert size & (size - 1) == 0
    return [1 << bit for bit in range(size.bit_length() - 1)]


def swapped(value, axis, reach):
    return lax.ppermute(value, axis, [(at, at ^ reach) for at in range(lax.axis_size(axis))])


def moved(value, distance):
    devices = range(lax.axis_size(AXES))
    return lax.ppermute(value, AXES, [(at, at + distance) for at in devices if at + distance in devices])


def local(locations, neighbours, observations, noise_prec):
    blocks, _, points = locations.shape
    fields = observations.shape[1]
    slots = neighbours.shape[1]
    assert blocks == 1
    coarse, groups = lax.axis_size("dev"), lax.axis_size("grp")
    sizes = (fields, points, coarse, slots)
    depth = len(slot_list(slots)) * points
    me = lax.axis_index(AXES).astype(jnp.int32).reshape(1)
    group = lax.axis_index("grp")
    smem, vmem = pltpu.SMEM, pltpu.VMEM
    square, tile = (points, points), (fields, points)

    (mine,) = call(pack_kernel, sizes, [(2 * fields, points)], [vmem, vmem])(locations, observations)
    before = moved(mine, 1)
    first = mine
    for reach in powers(groups):
        got = lax.ppermute(first, "grp", [(at, at + reach) for at in range(reach)])
        first = jnp.where((group >= reach) & (group < 2 * reach), got, first)
    table = first[None]
    reaches = powers(coarse)[::-1]
    for at, reach in enumerate(reaches):
        if at == 1:
            table, before = lax.optimization_barrier((table, before))
        if at == len(reaches) - 1:
            table, eliminated = lax.optimization_barrier((table, eliminated))
        got = swapped(table, "dev", reach)
        if at == 1:
            eliminated = call(near_kernel, sizes, [square] * 3, [smem, vmem, vmem])(neighbours, before, mine)
        table = jnp.concatenate([table, got], axis=0)
    part, near_own, near_prev, back, last = call(
        factor_kernel,
        sizes,
        [(coarse + 1,) + tile, tile, tile, (points, depth), square],
        [smem, smem] + [vmem] * 7,
        [pltpu.VMEM((slots, slots) + square, F32)],
    )(neighbours, me, before, mine, table, noise_prec, *eliminated)

    own_before, from_after = moved(near_own, 1), moved(near_prev, -1)
    for reach in powers(coarse):
        part = part + swapped(part, "dev", reach)
    part, own_before, from_after = lax.optimization_barrier((part, own_before, from_after))
    for reach in powers(groups):
        part = part + swapped(part, "grp", reach)
    sends, near_part, own_part, image, residual, ratios = call(
        step_kernel,
        sizes,
        [(coarse + 1,) + tile, tile, tile, tile, tile, (fields, LANES)],
        [smem, smem] + [vmem] * 11,
    )(neighbours, me, before, mine, table, noise_prec, part, near_own, near_prev, own_before, from_after, back, last)

    from_after = moved(near_part, -1)
    for reach in powers(coarse):
        kept = (sends.shape[0] - 1) // 2
        got = swapped(sends[kept:], "dev", reach)
        sends = jnp.concatenate([sends[:kept], sends[-1:]], axis=0) + got
    sends, from_after = lax.optimization_barrier((sends, from_after))
    for reach in powers(groups):
        sends = sends + swapped(sends, "grp", reach)
    return tuple(
        call(finish_kernel, sizes, [observations.shape] * 2, [smem] + [vmem] * 7)(
            me, sends, own_part, from_after, image, residual, ratios, observations
        )
    )


def solution(mesh):
    placed = (
        P(AXES, None, None),
        P(AXES, None),
        P(AXES, None, None),
        P(AXES, None, None),
    )
    return jax.shard_map(
        local,
        mesh=mesh,
        in_specs=placed,
        out_specs=(P(AXES, None, None), P(AXES, None, None)),
        check_vma=False,
    )
```

```python
import functools
import math

import jax
import jax.numpy as jnp
from jax import lax
from jax.experimental import pallas as pl
from jax.experimental.pallas import tpu as pltpu
from jax.sharding import PartitionSpec as P

SCALE_LENGTH = 0.5
NUGGET = 0.5
SQRT_THREE = math.sqrt(3.0)
LANES = 128
HIGHEST = lax.Precision.HIGHEST
F32 = jnp.float32
NN = (((1,), (0,)), ((), ()))
NT = (((1,), (1,)), ((), ()))
AXES = ("grp", "dev")
VMEM_LIMIT = 48 * 1024 * 1024


def split(value):
    high = value.astype(jnp.bfloat16)
    return high, (value - high.astype(F32)).astype(jnp.bfloat16)


def dot(left, right, dims=NN, precision=None):
    return lax.dot_general(left, right, dims, precision=precision, preferred_element_type=F32)


def dot_three(left, right, dims=NN):
    return dot(left[0], right[0], dims) + (dot(left[0], right[1], dims) + dot(left[1], right[0], dims))


def inverse(matrix, beside=()):
    order = matrix.shape[0]
    rows = lax.broadcasted_iota(jnp.int32, (order, order), 0)
    columns = lax.broadcasted_iota(jnp.int32, (order, order), 1)
    identity = (rows == columns).astype(F32)
    start = 2.0 / (2.0 * NUGGET + order)
    least = start * NUGGET
    ahead = start * matrix
    guess = None
    beside = list(beside)
    while True:
        reached = least * (2.0 - least)
        centre = 2.0 / (1.0 + reached)
        least = centre * reached
        ahead_parts = split(ahead)
        if guess is None:
            guess = (centre * start) * (2.0 * identity - ahead)
        else:
            guess = centre * (2.0 * guess - dot_three(split(guess), ahead_parts))
        if beside:
            beside.pop(0)()
        if 1.0 - least < 1e-3:
            break
        ahead = centre * (2.0 * ahead - dot_three(ahead_parts, ahead_parts))
    for work in beside:
        work()
    error = identity - dot(matrix, guess, precision=HIGHEST)
    return guess + dot_three(split(guess), split(error))


def slot_list(slots):
    return [slot for slot in range(slots) if slot != 1]


def mirrored(index, size):
    bits = size.bit_length() - 1
    return sum(((index >> bit) & 1) << (bits - 1 - bit) for bit in range(bits))


def covariance(first, second, alive, same):
    points = second.shape[1]
    rows_at_once = 64
    parts = []
    for start in range(0, points, rows_at_once):
        down = first[start : start + rows_at_once]
        total = None
        for k in range(3):
            offset = down[:, k : k + 1] - second[k : k + 1, :]
            total = offset * offset if total is None else total + offset * offset
        scaled = jnp.sqrt(total)
        value = (1.0 + scaled) * jnp.exp(-scaled) * alive
        if same:
            row = lax.broadcasted_iota(jnp.int32, value.shape, 0) + start
            column = lax.broadcasted_iota(jnp.int32, value.shape, 1)
            value = value + jnp.where(row == column, NUGGET * alive + (1.0 - alive), 0.0)
        parts.append(value)
    return jnp.concatenate(parts, axis=0)


def scaled_places(entry, fields):
    return entry[fields:] * (SQRT_THREE / SCALE_LENGTH)


def live_of(index):
    return (index >= 0).astype(F32)


def pack_kernel(sizes, locations, observed, packed):
    fields = sizes[0]
    packed[...] = jnp.zeros_like(packed)
    packed[:fields] = observed[0]
    packed[fields : fields + 3] = locations[0]


def factor_kernel(sizes, nbr, me, before, table, mine, noise, part, back_out, last_out, blocks):
    fields, points, coarse, slots = sizes
    used = slot_list(slots)
    own = len(used)
    ids = [nbr[0, slot] for slot in used] + [me[0]]
    here = lax.rem(me[0], coarse)
    entries = [before[0]]
    entries += [table[mirrored(jnp.maximum(index, 0) ^ here, coarse)] for index in ids[1:own]]
    entries += [mine[...]]
    live = [live_of(index) for index in ids]
    values = [entry[:fields] * alive for entry, alive in zip(entries, live)]
    places = [scaled_places(entry, fields) for entry in entries]
    turned = [jnp.transpose(place) for place in places]
    halves, lower, back = {}, {}, {}

    def build(i, j):
        blocks[i, j] = covariance(turned[i], places[j], live[i] * live[j], i == j)

    def parts_of(i, j):
        if (i, j) not in halves:
            halves[i, j] = split(blocks[i, j])
        return halves[i, j]

    def multiply(i, k, middle):
        lower[i, k] = dot(blocks[i, k], middle, precision=HIGHEST)

    def update(i, j, k):
        blocks[i, j] = blocks[i, j] - dot_three(split(lower[i, k]), parts_of(j, k), NT)

    def go_back(k):
        total = lower[own, k]
        for j in range(k + 1, own):
            total = total - dot_three(split(back[j]), split(lower[j, k]))
        back[k] = total

    build(0, 0)
    later = [functools.partial(build, i, j) for j in range(own + 1) for i in range(j, own + 1) if i > 0]
    for k in range(own):
        middle = inverse(blocks[k, k], later)
        for i in range(k + 1, own + 1):
            multiply(i, k, middle)
        update(k + 1, k + 1, k)
        later = [
            functools.partial(update, i, j, k)
            for j in range(k + 1, own + 1)
            for i in range(j, own + 1)
            if (i, j) != (k + 1, k + 1)
        ]
    last = inverse(blocks[own, own], [functools.partial(go_back, k) for k in range(own - 1, -1, -1)])
    for k in range(own):
        back_out[:, k * points : (k + 1) * points] = back[k]
    last_out[...] = last

    middle, spread, slot_parts = apply_block(values, back, last)
    own_part = spread + noise[0] * values[own]
    part[...] = jnp.zeros_like(part)
    product = jnp.sum(middle * spread + noise[0] * values[own] * values[own], axis=1, keepdims=True)
    square = jnp.sum(values[own] * values[own], axis=1, keepdims=True)
    part[coarse] = in_lanes([product, square], (fields, points))
    part[coarse + 1] = own_part
    part[coarse + 2] = slot_parts[0]
    for index, value in zip(ids, slot_parts + [own_part]):

        @pl.when((index >= 0) & (index < coarse))
        def _(index=index, value=value):
            part[index] = part[index] + value


def in_lanes(columns, shape):
    lane = lax.broadcasted_iota(jnp.int32, shape, 1)
    total = jnp.zeros(shape, F32)
    for at, column in enumerate(columns):
        total = jnp.where(lane == at, column, total)
    return total


def apply_block(values, back, last):
    own = len(values) - 1
    middle = values[own]
    for k in range(own):
        middle = middle - dot_three(split(values[k]), split(back[k]), NT)
    spread = dot_three(split(middle), split(last))
    spread_parts = split(spread)
    slot_parts = [-dot_three(spread_parts, split(back[k])) for k in range(own)]
    return middle, spread, slot_parts


def step_kernel(
    sizes, nbr, me, before, table, mine, noise, part, summed, shifted, back, last, sends, image_out, residual_out, ratio_out
):
    fields, points, coarse, slots = sizes
    used = slot_list(slots)
    own = len(used)
    ids = [nbr[0, slot] for slot in used] + [me[0]]
    here = lax.rem(me[0], coarse)
    product = summed[coarse][:, 0:1]
    norm_now = summed[coarse][:, 1:2]
    alpha = norm_now / product
    values = []
    for at, index in enumerate(ids):
        image = summed[jnp.clip(index, 0, coarse - 1)]
        if at == 0:
            observed = before[0, :fields]
            image = jnp.where(index < coarse, image, shifted[0] + part[coarse + 2])
        elif at == own:
            observed = mine[:fields]
            image = jnp.where(index < coarse, image, part[coarse + 1] + shifted[1])
        else:
            observed = table[mirrored(jnp.maximum(index, 0) ^ here, coarse)][:fields]
        values.append((observed - alpha * image) * live_of(index))
    back_parts = {k: back[:, k * points : (k + 1) * points] for k in range(own)}
    middle, spread, slot_parts = apply_block(values, back_parts, last[...])
    residual = values[own]
    inner = jnp.sum(middle * spread + noise[0] * residual * residual, axis=1, keepdims=True)
    cross = jnp.sum(residual * image, axis=1, keepdims=True)
    square = jnp.sum(residual * residual, axis=1, keepdims=True)
    sends[...] = jnp.zeros_like(sends)
    sends[coarse] = in_lanes([inner, cross, square], (fields, points))
    sends[coarse + 1] = slot_parts[0]
    for index, value in zip(ids[1:own], slot_parts[1:]):

        @pl.when(index >= 0)
        def _(index=index, value=value):
            place = mirrored(index ^ here, coarse)
            sends[place] = sends[place] + value

    image_out[0] = image
    image_out[1] = spread + noise[0] * residual
    residual_out[...] = residual
    ratio_out[...] = in_lanes([alpha, norm_now, product], (fields, LANES))


def finish_kernel(sizes, me, received, shifted, images, residual, ratios, mine, solution_out, residual_out):
    fields, points, coarse, slots = sizes
    owner = (me[0] < coarse).astype(F32)
    spread = images[1] + shifted[0] + owner * received[0]
    scalars = received[1]
    alpha, norm_first, product_first = ratios[:, 0:1], ratios[:, 1:2], ratios[:, 2:3]
    inner, cross, norm_now = scalars[:, 0:1], scalars[:, 1:2], scalars[:, 2:3]
    beta = norm_now / norm_first
    product = inner + beta * (2.0 * cross + beta * product_first)
    step = norm_now / product
    observed = mine[:fields]
    direction = residual[...] + beta * observed
    solution_out[0] = alpha * observed + step * direction
    residual_out[0] = residual[...] - step * (spread + beta * images[0])


def call(kernel, sizes, outs, in_spaces, scratch=()):
    return pl.pallas_call(
        functools.partial(kernel, sizes),
        out_shape=[jax.ShapeDtypeStruct(shape, F32) for shape in outs],
        in_specs=[pl.BlockSpec(memory_space=space) for space in in_spaces],
        out_specs=[pl.BlockSpec(memory_space=pltpu.VMEM)] * len(outs),
        scratch_shapes=list(scratch),
        compiler_params=pltpu.CompilerParams(vmem_limit_bytes=VMEM_LIMIT),
    )


def powers(size):
    assert size & (size - 1) == 0
    return [1 << bit for bit in range(size.bit_length() - 1)]


def swapped(value, axis, reach):
    return lax.ppermute(value, axis, [(at, at ^ reach) for at in range(lax.axis_size(axis))])


def exchanges():
    steps, bit = [], 0
    for axis in AXES[::-1]:
        for reach in powers(lax.axis_size(axis)):
            steps.append((axis, reach, bit))
            bit += 1
    return steps


def carry(shifted, ends, got, me, bit, kinds):
    low, upper = me & ((1 << bit) - 1), ((me >> bit) & 1) == 1
    new_shifted, new_ends = [], []
    for at, kind in enumerate(kinds):
        if kind == 1:
            takes, keeps = upper & (low == 0), upper
        else:
            takes, keeps = ~upper & (low == (1 << bit) - 1), ~upper
        new_shifted.append(jnp.where(takes, got[at], shifted[at]))
        new_ends.append(jnp.where(keeps, ends[at], got[at]))
    return jnp.stack(new_shifted), jnp.stack(new_ends)


def local(locations, neighbours, observations, noise_prec):
    blocks, _, points = locations.shape
    fields = observations.shape[1]
    slots = neighbours.shape[1]
    assert blocks == 1
    coarse = lax.axis_size("dev")
    sizes = (fields, points, coarse, slots)
    depth = len(slot_list(slots)) * points
    me = lax.axis_index(AXES).astype(jnp.int32)
    group = lax.axis_index("grp")
    smem, vmem = pltpu.SMEM, pltpu.VMEM
    square, tile = (points, points), (fields, points)
    steps = exchanges()

    (mine,) = call(pack_kernel, sizes, [(2 * fields, points)], [vmem, vmem])(locations, observations)
    before, table = mine[None], mine[None]
    for axis, reach, bit in steps[::-1]:
        got = swapped(jnp.concatenate([table, before], axis=0), axis, reach)
        low = (1 << bit) - 1
        before = jnp.where((me & low) == low, got[-1:], before)
        if axis == "grp":
            table = jnp.where((group & reach) != 0, got[:-1], table)
        else:
            table = jnp.concatenate([table, got[:-1]], axis=0)
    at = me.reshape(1)
    part, back, last = call(
        factor_kernel,
        sizes,
        [(coarse + 3,) + tile, (points, depth), square],
        [smem, smem] + [vmem] * 4,
        [pltpu.VMEM((slots, slots) + square, F32)],
    )(neighbours, at, before, table, mine, noise_prec)

    summed, ends, shifted = part[:-2], part[-2:], jnp.zeros_like(part[-2:])
    for axis, reach, bit in steps:
        got = swapped(jnp.concatenate([summed, ends], axis=0), axis, reach)
        summed = summed + got[:-2]
        shifted, ends = carry(shifted, ends, got[-2:], me, bit, (1, -1))
    sends, images, residual, ratios = call(
        step_kernel,
        sizes,
        [(coarse + 2,) + tile, (2,) + tile, tile, (fields, LANES)],
        [smem, smem] + [vmem] * 9,
    )(neighbours, at, before, table, mine, noise_prec, part, summed, shifted, back, last)

    summed, ends, shifted = sends[:-1], sends[-1:], jnp.zeros_like(sends[-1:])
    for axis, reach, bit in steps:
        kept = (summed.shape[0] - 1) // 2 if axis == "dev" else 0
        got = swapped(jnp.concatenate([summed[kept:], ends], axis=0), axis, reach)
        if axis == "dev":
            summed = jnp.concatenate([summed[:kept], summed[-1:]], axis=0)
        summed = summed + got[:-1]
        shifted, ends = carry(shifted, ends, got[-1:], me, bit, (-1,))
    return tuple(
        call(finish_kernel, sizes, [observations.shape] * 2, [smem] + [vmem] * 6)(
            at, summed, shifted, images, residual, ratios, mine
        )
    )


def solution(mesh):
    placed = (
        P(AXES, None, None),
        P(AXES, None),
        P(AXES, None, None),
        P(AXES, None, None),
    )
    return jax.shard_map(
        local,
        mesh=mesh,
        in_specs=placed,
        out_specs=(P(AXES, None, None), P(AXES, None, None)),
        check_vma=False,
    )
```

```python
import functools
import math

import jax
import jax.numpy as jnp
from jax import lax
from jax.experimental import pallas as pl
from jax.experimental.pallas import tpu as pltpu
from jax.sharding import PartitionSpec as P

SCALE_LENGTH = 0.5
NUGGET = 0.5
SQRT_THREE = math.sqrt(3.0)
LANES = 128
HIGHEST = lax.Precision.HIGHEST
F32 = jnp.float32
NN = (((1,), (0,)), ((), ()))
NT = (((1,), (1,)), ((), ()))
AXES = ("grp", "dev")
VMEM_LIMIT = 48 * 1024 * 1024
CLOSE = 2e-3
ALWAYS = 3


def split(value):
    high = value.astype(jnp.bfloat16)
    return high, (value - high.astype(F32)).astype(jnp.bfloat16)


def dot(left, right, dims=NN, precision=None):
    return lax.dot_general(left, right, dims, precision=precision, preferred_element_type=F32)


def dot_three(left, right, dims=NN):
    return dot(left[0], right[0], dims) + (dot(left[0], right[1], dims) + dot(left[1], right[0], dims))


def split_fine(value):
    high = value.astype(jnp.bfloat16)
    rest = value - high.astype(F32)
    middle = rest.astype(jnp.bfloat16)
    return high, middle, (rest - middle.astype(F32)).astype(jnp.bfloat16)


def dot_six(left, right, dims=NN):
    small = dot(left[1], right[1], dims) + (dot(left[0], right[2], dims) + dot(left[2], right[0], dims))
    return dot(left[0], right[0], dims) + ((dot(left[0], right[1], dims) + dot(left[1], right[0], dims)) + small)


def newton_levels(order):
    least = 1.0 - CLOSE
    levels = [(1.0, 1.0 / least - NUGGET)]
    while levels[-1][1] < order + NUGGET:
        reached = least / (2.0 - least)
        least = 1.0 - math.sqrt(1.0 - reached)
        levels.append((2.0 / (1.0 + reached), 1.0 / least - NUGGET))
    return levels


def inverse(matrix, ahead, guess):
    order = matrix.shape[0]
    rows = lax.broadcasted_iota(jnp.int32, (order, order), 0)
    columns = lax.broadcasted_iota(jnp.int32, (order, order), 1)
    identity = (rows == columns).astype(F32)
    levels = newton_levels(order)
    always = min(ALWAYS, len(levels) - 1)
    bound = jnp.minimum(jnp.max(jnp.sum(jnp.abs(matrix), axis=0)), order + NUGGET)
    start = 2.0 / (NUGGET + levels[always][1])
    for level in range(always + 1, len(levels)):
        start = jnp.where(bound > levels[level - 1][1], 2.0 / (NUGGET + levels[level][1]), start)
    ahead[...] = start * matrix
    guess[...] = start * identity

    def advance(scale, now, held, only_guess=False):
        now_parts = split(now)
        new_held = scale * (2.0 * held - dot_three(split(held), now_parts))
        return (None if only_guess else scale * (2.0 * now - dot_three(now_parts, now_parts))), new_held

    for level in range(len(levels) - 1, always, -1):

        @pl.when(bound > levels[level - 1][1])
        def _(scale=levels[level][0]):
            ahead[...], guess[...] = advance(scale, ahead[...], guess[...])

    now, held = ahead[...], guess[...]
    for level in range(always, 0, -1):
        now, held = advance(levels[level][0], now, held, level == 1)
    error = identity - dot_six(split_fine(matrix), split_fine(held))
    return held + dot_three(split(held), split(error))


def slot_list(slots):
    return [slot for slot in range(slots) if slot != 1]


def mirrored(index, size):
    bits = size.bit_length() - 1
    return sum(((index >> bit) & 1) << (bits - 1 - bit) for bit in range(bits))


def covariance(first, second, alive, same):
    points = second.shape[1]
    rows_at_once = 64
    parts = []
    for start in range(0, points, rows_at_once):
        down = first[start : start + rows_at_once]
        total = None
        for k in range(3):
            offset = down[:, k : k + 1] - second[k : k + 1, :]
            total = offset * offset if total is None else total + offset * offset
        scaled = jnp.sqrt(total)
        value = (1.0 + scaled) * jnp.exp(-scaled) * alive
        if same:
            row = lax.broadcasted_iota(jnp.int32, value.shape, 0) + start
            column = lax.broadcasted_iota(jnp.int32, value.shape, 1)
            value = value + jnp.where(row == column, NUGGET * alive + (1.0 - alive), 0.0)
        parts.append(value)
    return jnp.concatenate(parts, axis=0)


def scaled_places(entry, fields):
    return entry[fields:] * (SQRT_THREE / SCALE_LENGTH)


def live_of(index):
    return (index >= 0).astype(F32)


def pack_kernel(sizes, locations, observed, packed):
    fields = sizes[0]
    packed[...] = jnp.zeros_like(packed)
    packed[:fields] = observed[0]
    packed[fields : fields + 3] = locations[0]


def factor_kernel(sizes, nbr, me, before, table, mine, noise, part, back_out, last_out, columns, lower, ahead, guess):
    fields, points, coarse, slots = sizes
    used = slot_list(slots)
    own = len(used)
    ids = [nbr[0, slot] for slot in used] + [me[0]]
    here = lax.rem(me[0], coarse)
    entries = [before[0]]
    entries += [table[mirrored(jnp.maximum(index, 0) ^ here, coarse)] for index in ids[1:own]]
    entries += [mine[...]]
    live = [live_of(index) for index in ids]
    values = [entry[:fields] * alive for entry, alive in zip(entries, live)]
    places = [scaled_places(entry, fields) for entry in entries]
    turned = [jnp.transpose(place) for place in places]

    def at(i, end=None):
        return pl.ds(i * points, ((i + 1 if end is None else end) - i) * points)

    for j in range(own + 1):
        for i in range(j, own + 1):
            columns[j, at(i)] = covariance(turned[i], places[j], live[i] * live[j], i == j)
    for k in range(own):
        middle = inverse(columns[k, at(k)], ahead, guess)
        side = columns[k, at(k + 1, own + 1)]
        below = dot_six(split_fine(side), split_fine(middle))
        lower[k, at(k + 1, own + 1)] = below
        side_parts, below_parts = split(side), split(below)
        for j in range(k + 1, own + 1):
            cut = (j - k - 1) * points
            left = [piece[cut:] for piece in below_parts]
            right = [piece[cut : cut + points] for piece in side_parts]
            columns[j, at(j, own + 1)] = columns[j, at(j, own + 1)] - dot_three(left, right, NT)
    for k in range(own - 1, -1, -1):
        total = lower[k, at(own)]
        if k + 1 < own:
            done = back_out[:, (k + 1) * points :]
            total = total - dot_three(split(done), split(lower[k, at(k + 1, own)]))
        back_out[:, k * points : (k + 1) * points] = total
    last = inverse(columns[own, at(own)], ahead, guess)
    last_out[...] = last
    back = {k: back_out[:, k * points : (k + 1) * points] for k in range(own)}

    middle, spread, slot_parts = apply_block(values, back, last)
    own_part = spread + noise[0] * values[own]
    part[...] = jnp.zeros_like(part)
    product = jnp.sum(middle * spread + noise[0] * values[own] * values[own], axis=1, keepdims=True)
    square = jnp.sum(values[own] * values[own], axis=1, keepdims=True)
    part[coarse] = in_lanes([product, square], (fields, points))
    part[coarse + 1] = own_part
    part[coarse + 2] = slot_parts[0]
    for index, value in zip(ids, slot_parts + [own_part]):

        @pl.when((index >= 0) & (index < coarse))
        def _(index=index, value=value):
            part[index] = part[index] + value


def in_lanes(columns, shape):
    lane = lax.broadcasted_iota(jnp.int32, shape, 1)
    total = jnp.zeros(shape, F32)
    for at, column in enumerate(columns):
        total = jnp.where(lane == at, column, total)
    return total


def apply_block(values, back, last):
    own = len(values) - 1
    middle = values[own]
    for k in range(own):
        middle = middle - dot_three(split(values[k]), split(back[k]), NT)
    spread = dot_three(split(middle), split(last))
    spread_parts = split(spread)
    slot_parts = [-dot_three(spread_parts, split(back[k])) for k in range(own)]
    return middle, spread, slot_parts


def step_kernel(
    sizes, nbr, me, before, table, mine, noise, part, summed, shifted, back, last, sends, image_out, residual_out, ratio_out
):
    fields, points, coarse, slots = sizes
    used = slot_list(slots)
    own = len(used)
    ids = [nbr[0, slot] for slot in used] + [me[0]]
    here = lax.rem(me[0], coarse)
    product = summed[coarse][:, 0:1]
    norm_now = summed[coarse][:, 1:2]
    alpha = norm_now / product
    values = []
    for at, index in enumerate(ids):
        image = summed[jnp.clip(index, 0, coarse - 1)]
        if at == 0:
            observed = before[0, :fields]
            image = jnp.where(index < coarse, image, shifted[0] + part[coarse + 2])
        elif at == own:
            observed = mine[:fields]
            image = jnp.where(index < coarse, image, part[coarse + 1] + shifted[1])
        else:
            observed = table[mirrored(jnp.maximum(index, 0) ^ here, coarse)][:fields]
        values.append((observed - alpha * image) * live_of(index))
    back_parts = {k: back[:, k * points : (k + 1) * points] for k in range(own)}
    middle, spread, slot_parts = apply_block(values, back_parts, last[...])
    residual = values[own]
    inner = jnp.sum(middle * spread + noise[0] * residual * residual, axis=1, keepdims=True)
    cross = jnp.sum(residual * image, axis=1, keepdims=True)
    square = jnp.sum(residual * residual, axis=1, keepdims=True)
    sends[...] = jnp.zeros_like(sends)
    sends[coarse] = in_lanes([inner, cross, square], (fields, points))
    sends[coarse + 1] = slot_parts[0]
    for index, value in zip(ids[1:own], slot_parts[1:]):

        @pl.when(index >= 0)
        def _(index=index, value=value):
            place = mirrored(index ^ here, coarse)
            sends[place] = sends[place] + value

    image_out[0] = image
    image_out[1] = spread + noise[0] * residual
    residual_out[...] = residual
    ratio_out[...] = in_lanes([alpha, norm_now, product], (fields, LANES))


def finish_kernel(sizes, me, received, shifted, images, residual, ratios, mine, solution_out, residual_out):
    fields, points, coarse, slots = sizes
    owner = (me[0] < coarse).astype(F32)
    spread = images[1] + shifted[0] + owner * received[0]
    scalars = received[1]
    alpha, norm_first, product_first = ratios[:, 0:1], ratios[:, 1:2], ratios[:, 2:3]
    inner, cross, norm_now = scalars[:, 0:1], scalars[:, 1:2], scalars[:, 2:3]
    beta = norm_now / norm_first
    product = inner + beta * (2.0 * cross + beta * product_first)
    step = norm_now / product
    observed = mine[:fields]
    direction = residual[...] + beta * observed
    solution_out[0] = alpha * observed + step * direction
    residual_out[0] = residual[...] - step * (spread + beta * images[0])


def call(kernel, sizes, outs, in_spaces, scratch=()):
    return pl.pallas_call(
        functools.partial(kernel, sizes),
        out_shape=[jax.ShapeDtypeStruct(shape, F32) for shape in outs],
        in_specs=[pl.BlockSpec(memory_space=space) for space in in_spaces],
        out_specs=[pl.BlockSpec(memory_space=pltpu.VMEM)] * len(outs),
        scratch_shapes=list(scratch),
        compiler_params=pltpu.CompilerParams(vmem_limit_bytes=VMEM_LIMIT),
    )


def powers(size):
    assert size & (size - 1) == 0
    return [1 << bit for bit in range(size.bit_length() - 1)]


def swapped(value, axis, reach):
    return lax.ppermute(value, axis, [(at, at ^ reach) for at in range(lax.axis_size(axis))])


def exchanges():
    steps, bit = [], 0
    for axis in AXES[::-1]:
        for reach in powers(lax.axis_size(axis)):
            steps.append((axis, reach, bit))
            bit += 1
    return steps


def carry(shifted, ends, got, me, bit, kinds):
    low, upper = me & ((1 << bit) - 1), ((me >> bit) & 1) == 1
    new_shifted, new_ends = [], []
    for at, kind in enumerate(kinds):
        if kind == 1:
            takes, keeps = upper & (low == 0), upper
        else:
            takes, keeps = ~upper & (low == (1 << bit) - 1), ~upper
        new_shifted.append(jnp.where(takes, got[at], shifted[at]))
        new_ends.append(jnp.where(keeps, ends[at], got[at]))
    return jnp.stack(new_shifted), jnp.stack(new_ends)


def local(locations, neighbours, observations, noise_prec):
    blocks, _, points = locations.shape
    fields = observations.shape[1]
    slots = neighbours.shape[1]
    assert blocks == 1
    coarse = lax.axis_size("dev")
    sizes = (fields, points, coarse, slots)
    depth = len(slot_list(slots)) * points
    me = lax.axis_index(AXES).astype(jnp.int32)
    group = lax.axis_index("grp")
    smem, vmem = pltpu.SMEM, pltpu.VMEM
    square, tile = (points, points), (fields, points)
    steps = exchanges()

    (mine,) = call(pack_kernel, sizes, [(2 * fields, points)], [vmem, vmem])(locations, observations)
    before, table = mine[None], mine[None]
    for axis, reach, bit in steps[::-1]:
        got = swapped(jnp.concatenate([table, before], axis=0), axis, reach)
        low = (1 << bit) - 1
        before = jnp.where((me & low) == low, got[-1:], before)
        if axis == "grp":
            table = jnp.where((group & reach) != 0, got[:-1], table)
        else:
            table = jnp.concatenate([table, got[:-1]], axis=0)
    at = me.reshape(1)
    part, back, last = call(
        factor_kernel,
        sizes,
        [(coarse + 3,) + tile, (points, depth), square],
        [smem, smem] + [vmem] * 4,
        [pltpu.VMEM((slots, slots * points, points), F32)] * 2 + [pltpu.VMEM(square, F32)] * 2,
    )(neighbours, at, before, table, mine, noise_prec)

    summed, ends, shifted = part[:-2], part[-2:], jnp.zeros_like(part[-2:])
    for axis, reach, bit in steps:
        got = swapped(jnp.concatenate([summed, ends], axis=0), axis, reach)
        summed = summed + got[:-2]
        shifted, ends = carry(shifted, ends, got[-2:], me, bit, (1, -1))
    sends, images, residual, ratios = call(
        step_kernel,
        sizes,
        [(coarse + 2,) + tile, (2,) + tile, tile, (fields, LANES)],
        [smem, smem] + [vmem] * 9,
    )(neighbours, at, before, table, mine, noise_prec, part, summed, shifted, back, last)

    summed, ends, shifted = sends[:-1], sends[-1:], jnp.zeros_like(sends[-1:])
    for axis, reach, bit in steps:
        kept = (summed.shape[0] - 1) // 2 if axis == "dev" else 0
        got = swapped(jnp.concatenate([summed[kept:], ends], axis=0), axis, reach)
        if axis == "dev":
            summed = jnp.concatenate([summed[:kept], summed[-1:]], axis=0)
        summed = summed + got[:-1]
        shifted, ends = carry(shifted, ends, got[-1:], me, bit, (-1,))
    return tuple(
        call(finish_kernel, sizes, [observations.shape] * 2, [smem] + [vmem] * 6)(
            at, summed, shifted, images, residual, ratios, mine
        )
    )


def solution(mesh):
    placed = (
        P(AXES, None, None),
        P(AXES, None),
        P(AXES, None, None),
        P(AXES, None, None),
    )
    return jax.shard_map(
        local,
        mesh=mesh,
        in_specs=placed,
        out_specs=(P(AXES, None, None), P(AXES, None, None)),
        check_vma=False,
    )
```

```python
import functools
import math

import jax
import jax.numpy as jnp
from jax import lax
from jax.experimental import pallas as pl
from jax.experimental.pallas import tpu as pltpu
from jax.sharding import PartitionSpec as P

SCALE_LENGTH = 0.5
NUGGET = 0.5
SQRT_THREE = math.sqrt(3.0)
LANES = 128
HIGHEST = lax.Precision.HIGHEST
F32 = jnp.float32
NN = (((1,), (0,)), ((), ()))
NT = (((1,), (1,)), ((), ()))
AXES = ("grp", "dev")
VMEM_LIMIT = 48 * 1024 * 1024
CLOSE = 2e-3
ALWAYS = 3
ROWS = 128


def split(value):
    high = value.astype(jnp.bfloat16)
    return high, (value - high.astype(F32)).astype(jnp.bfloat16)


def dot(left, right, dims=NN, precision=None):
    return lax.dot_general(left, right, dims, precision=precision, preferred_element_type=F32)


def split_fine(value):
    high = value.astype(jnp.bfloat16)
    rest = value - high.astype(F32)
    middle = rest.astype(jnp.bfloat16)
    return high, middle, (rest - middle.astype(F32)).astype(jnp.bfloat16)


def taken(base, left, right, dims=NN, rows=None):
    count = len(left)
    pieces = []
    rows = rows or base.shape[0]
    for first in range(0, base.shape[0], rows):
        total = base[first : first + rows]
        cut = [part[first : first + rows] for part in left]
        for at in range(count):
            group = None
            for other in range(count - 1 - at, -1, -1):
                term = dot(cut[other], right[at], dims)
                group = term if group is None else group + term
            total = total - group
        pieces.append(total)
    return pieces[0] if len(pieces) == 1 else jnp.concatenate(pieces, axis=0)


def newton_levels(order):
    least = 1.0 - CLOSE
    levels = [(1.0, 1.0 / least - NUGGET)]
    while levels[-1][1] < order + NUGGET:
        reached = least / (2.0 - least)
        least = 1.0 - math.sqrt(1.0 - reached)
        levels.append((2.0 / (1.0 + reached), 1.0 / least - NUGGET))
    return levels


def inverse(matrix, ahead, guess):
    order = matrix.shape[0]
    rows = lax.broadcasted_iota(jnp.int32, (order, order), 0)
    columns = lax.broadcasted_iota(jnp.int32, (order, order), 1)
    identity = (rows == columns).astype(F32)
    levels = newton_levels(order)
    always = min(ALWAYS, len(levels) - 1)
    bound = jnp.minimum(jnp.max(jnp.sum(jnp.abs(matrix), axis=0)), order + NUGGET)
    start = 2.0 / (NUGGET + levels[always][1])
    for level in range(always + 1, len(levels)):
        start = jnp.where(bound > levels[level - 1][1], 2.0 / (NUGGET + levels[level][1]), start)
    ahead[...] = start * matrix
    guess[...] = start * identity

    def advance(scale, now, held, only_guess=False):
        now_parts = split(now)
        new_held = scale * taken(2.0 * held, split(held), now_parts, rows=ROWS)
        return (None if only_guess else scale * taken(2.0 * now, now_parts, now_parts, rows=ROWS)), new_held

    for level in range(len(levels) - 1, always, -1):

        @pl.when(bound > levels[level - 1][1])
        def _(scale=levels[level][0]):
            ahead[...], guess[...] = advance(scale, ahead[...], guess[...])

    now, held = ahead[...], guess[...]
    for level in range(always, 0, -1):
        now, held = advance(levels[level][0], now, held, level == 1)
    error = taken(identity, split_fine(matrix), split_fine(held), rows=ROWS)
    return taken(held, split(held), split(-error), rows=ROWS)


def slot_list(slots):
    return [slot for slot in range(slots) if slot != 1]


def mirrored(index, size):
    bits = size.bit_length() - 1
    return sum(((index >> bit) & 1) << (bits - 1 - bit) for bit in range(bits))


def covariance(first, second, alive, same):
    points = second.shape[1]
    rows_at_once = 64
    parts = []
    for start in range(0, points, rows_at_once):
        down = first[start : start + rows_at_once]
        total = None
        for k in range(3):
            offset = down[:, k : k + 1] - second[k : k + 1, :]
            total = offset * offset if total is None else total + offset * offset
        scaled = jnp.sqrt(total)
        value = (1.0 + scaled) * jnp.exp(-scaled) * alive
        if same:
            row = lax.broadcasted_iota(jnp.int32, value.shape, 0) + start
            column = lax.broadcasted_iota(jnp.int32, value.shape, 1)
            value = value + jnp.where(row == column, NUGGET * alive + (1.0 - alive), 0.0)
        parts.append(value)
    return jnp.concatenate(parts, axis=0)


def scaled_places(entry, fields):
    return entry[fields:] * (SQRT_THREE / SCALE_LENGTH)


def live_of(index):
    return (index >= 0).astype(F32)


def pack_kernel(sizes, locations, observed, packed):
    fields = sizes[0]
    packed[...] = jnp.zeros_like(packed)
    packed[:fields] = observed[0]
    packed[fields : fields + 3] = locations[0]


def factor_kernel(sizes, nbr, me, before, table, mine, noise, part, back_out, last_out, columns, lower, ahead, guess):
    fields, points, coarse, slots = sizes
    used = slot_list(slots)
    own = len(used)
    ids = [nbr[0, slot] for slot in used] + [me[0]]
    here = lax.rem(me[0], coarse)
    entries = [before[0]]
    entries += [table[mirrored(jnp.maximum(index, 0) ^ here, coarse)] for index in ids[1:own]]
    entries += [mine[...]]
    live = [live_of(index) for index in ids]
    values = [entry[:fields] * alive for entry, alive in zip(entries, live)]
    places = [scaled_places(entry, fields) for entry in entries]
    turned = [jnp.transpose(place) for place in places]

    def at(i, end=None):
        return pl.ds(i * points, ((i + 1 if end is None else end) - i) * points)

    for j in range(own + 1):
        for i in range(j, own + 1):
            columns[j, at(i)] = covariance(turned[i], places[j], live[i] * live[j], i == j)
    for k in range(own):
        middle = inverse(columns[k, at(k)], ahead, guess)
        side = columns[k, at(k + 1, own + 1)]
        below = -taken(jnp.zeros_like(side), split_fine(side), split_fine(middle))
        lower[k, at(k + 1, own + 1)] = below
        side_parts, below_parts = split(side), split(below)
        for j in range(k + 1, own + 1):
            cut = (j - k - 1) * points
            left = [piece[cut:] for piece in below_parts]
            right = [piece[cut : cut + points] for piece in side_parts]
            columns[j, at(j, own + 1)] = taken(columns[j, at(j, own + 1)], left, right, NT)
    for k in range(own - 1, -1, -1):
        total = lower[k, at(own)]
        if k + 1 < own:
            done = back_out[:, (k + 1) * points :]
            total = taken(total, split(done), split(lower[k, at(k + 1, own)]))
        back_out[:, k * points : (k + 1) * points] = total
    last = inverse(columns[own, at(own)], ahead, guess)
    last_out[...] = last
    back = {k: back_out[:, k * points : (k + 1) * points] for k in range(own)}

    middle, spread, slot_parts = apply_block(values, back, last)
    own_part = spread + noise[0] * values[own]
    part[...] = jnp.zeros_like(part)
    product = jnp.sum(middle * spread + noise[0] * values[own] * values[own], axis=1, keepdims=True)
    square = jnp.sum(values[own] * values[own], axis=1, keepdims=True)
    part[coarse] = in_lanes([product, square], (fields, points))
    part[coarse + 1] = own_part
    part[coarse + 2] = slot_parts[0]
    for index, value in zip(ids, slot_parts + [own_part]):

        @pl.when((index >= 0) & (index < coarse))
        def _(index=index, value=value):
            part[index] = part[index] + value


def in_lanes(columns, shape):
    lane = lax.broadcasted_iota(jnp.int32, shape, 1)
    total = jnp.zeros(shape, F32)
    for at, column in enumerate(columns):
        total = jnp.where(lane == at, column, total)
    return total


def apply_block(values, back, last):
    own = len(values) - 1
    middle = values[own]
    for k in range(own):
        middle = taken(middle, split(values[k]), split(back[k]), NT)
    spread = -taken(jnp.zeros_like(middle), split(middle), split(last))
    spread_parts = split(spread)
    slot_parts = [taken(jnp.zeros_like(middle), spread_parts, split(back[k])) for k in range(own)]
    return middle, spread, slot_parts


def step_kernel(
    sizes, nbr, me, before, table, mine, noise, part, summed, shifted, back, last, sends, image_out, residual_out, ratio_out
):
    fields, points, coarse, slots = sizes
    used = slot_list(slots)
    own = len(used)
    ids = [nbr[0, slot] for slot in used] + [me[0]]
    here = lax.rem(me[0], coarse)
    product = summed[coarse][:, 0:1]
    norm_now = summed[coarse][:, 1:2]
    alpha = norm_now / product
    values = []
    for at, index in enumerate(ids):
        image = summed[jnp.clip(index, 0, coarse - 1)]
        if at == 0:
            observed = before[0, :fields]
            image = jnp.where(index < coarse, image, shifted[0] + part[coarse + 2])
        elif at == own:
            observed = mine[:fields]
            image = jnp.where(index < coarse, image, part[coarse + 1] + shifted[1])
        else:
            observed = table[mirrored(jnp.maximum(index, 0) ^ here, coarse)][:fields]
        values.append((observed - alpha * image) * live_of(index))
    back_parts = {k: back[:, k * points : (k + 1) * points] for k in range(own)}
    middle, spread, slot_parts = apply_block(values, back_parts, last[...])
    residual = values[own]
    inner = jnp.sum(middle * spread + noise[0] * residual * residual, axis=1, keepdims=True)
    cross = jnp.sum(residual * image, axis=1, keepdims=True)
    square = jnp.sum(residual * residual, axis=1, keepdims=True)
    sends[...] = jnp.zeros_like(sends)
    sends[coarse] = in_lanes([inner, cross, square], (fields, points))
    sends[coarse + 1] = slot_parts[0]
    for index, value in zip(ids[1:own], slot_parts[1:]):

        @pl.when(index >= 0)
        def _(index=index, value=value):
            place = mirrored(index ^ here, coarse)
            sends[place] = sends[place] + value

    image_out[0] = image
    image_out[1] = spread + noise[0] * residual
    residual_out[...] = residual
    ratio_out[...] = in_lanes([alpha, norm_now, product], (fields, LANES))


def finish_kernel(sizes, me, received, shifted, images, residual, ratios, mine, solution_out, residual_out):
    fields, points, coarse, slots = sizes
    owner = (me[0] < coarse).astype(F32)
    spread = images[1] + shifted[0] + owner * received[0]
    scalars = received[1]
    alpha, norm_first, product_first = ratios[:, 0:1], ratios[:, 1:2], ratios[:, 2:3]
    inner, cross, norm_now = scalars[:, 0:1], scalars[:, 1:2], scalars[:, 2:3]
    beta = norm_now / norm_first
    product = inner + beta * (2.0 * cross + beta * product_first)
    step = norm_now / product
    observed = mine[:fields]
    direction = residual[...] + beta * observed
    solution_out[0] = alpha * observed + step * direction
    residual_out[0] = residual[...] - step * (spread + beta * images[0])


def call(kernel, sizes, outs, in_spaces, scratch=()):
    return pl.pallas_call(
        functools.partial(kernel, sizes),
        out_shape=[jax.ShapeDtypeStruct(shape, F32) for shape in outs],
        in_specs=[pl.BlockSpec(memory_space=space) for space in in_spaces],
        out_specs=[pl.BlockSpec(memory_space=pltpu.VMEM)] * len(outs),
        scratch_shapes=list(scratch),
        compiler_params=pltpu.CompilerParams(vmem_limit_bytes=VMEM_LIMIT),
    )


def powers(size):
    assert size & (size - 1) == 0
    return [1 << bit for bit in range(size.bit_length() - 1)]


def swapped(value, axis, reach):
    return lax.ppermute(value, axis, [(at, at ^ reach) for at in range(lax.axis_size(axis))])


def exchanges():
    steps, bit = [], 0
    for axis in AXES[::-1]:
        for reach in powers(lax.axis_size(axis)):
            steps.append((axis, reach, bit))
            bit += 1
    return steps


def carry(shifted, ends, got, me, bit, kinds):
    low, upper = me & ((1 << bit) - 1), ((me >> bit) & 1) == 1
    new_shifted, new_ends = [], []
    for at, kind in enumerate(kinds):
        if kind == 1:
            takes, keeps = upper & (low == 0), upper
        else:
            takes, keeps = ~upper & (low == (1 << bit) - 1), ~upper
        new_shifted.append(jnp.where(takes, got[at], shifted[at]))
        new_ends.append(jnp.where(keeps, ends[at], got[at]))
    return jnp.stack(new_shifted), jnp.stack(new_ends)


def local(locations, neighbours, observations, noise_prec):
    blocks, _, points = locations.shape
    fields = observations.shape[1]
    slots = neighbours.shape[1]
    assert blocks == 1
    coarse = lax.axis_size("dev")
    sizes = (fields, points, coarse, slots)
    depth = len(slot_list(slots)) * points
    me = lax.axis_index(AXES).astype(jnp.int32)
    group = lax.axis_index("grp")
    smem, vmem = pltpu.SMEM, pltpu.VMEM
    square, tile = (points, points), (fields, points)
    steps = exchanges()

    (mine,) = call(pack_kernel, sizes, [(2 * fields, points)], [vmem, vmem])(locations, observations)
    before, table = mine[None], mine[None]
    for axis, reach, bit in steps[::-1]:
        got = swapped(jnp.concatenate([table, before], axis=0), axis, reach)
        low = (1 << bit) - 1
        before = jnp.where((me & low) == low, got[-1:], before)
        if axis == "grp":
            table = jnp.where((group & reach) != 0, got[:-1], table)
        else:
            table = jnp.concatenate([table, got[:-1]], axis=0)
    at = me.reshape(1)
    part, back, last = call(
        factor_kernel,
        sizes,
        [(coarse + 3,) + tile, (points, depth), square],
        [smem, smem] + [vmem] * 4,
        [pltpu.VMEM((slots, slots * points, points), F32)] * 2 + [pltpu.VMEM(square, F32)] * 2,
    )(neighbours, at, before, table, mine, noise_prec)

    summed, ends, shifted = part[:-2], part[-2:], jnp.zeros_like(part[-2:])
    for axis, reach, bit in steps:
        got = swapped(jnp.concatenate([summed, ends], axis=0), axis, reach)
        summed = summed + got[:-2]
        shifted, ends = carry(shifted, ends, got[-2:], me, bit, (1, -1))
    sends, images, residual, ratios = call(
        step_kernel,
        sizes,
        [(coarse + 2,) + tile, (2,) + tile, tile, (fields, LANES)],
        [smem, smem] + [vmem] * 9,
    )(neighbours, at, before, table, mine, noise_prec, part, summed, shifted, back, last)

    summed, ends, shifted = sends[:-1], sends[-1:], jnp.zeros_like(sends[-1:])
    for axis, reach, bit in steps:
        kept = (summed.shape[0] - 1) // 2 if axis == "dev" else 0
        got = swapped(jnp.concatenate([summed[kept:], ends], axis=0), axis, reach)
        if axis == "dev":
            summed = jnp.concatenate([summed[:kept], summed[-1:]], axis=0)
        summed = summed + got[:-1]
        shifted, ends = carry(shifted, ends, got[-1:], me, bit, (-1,))
    return tuple(
        call(finish_kernel, sizes, [observations.shape] * 2, [smem] + [vmem] * 6)(
            at, summed, shifted, images, residual, ratios, mine
        )
    )


def solution(mesh):
    placed = (
        P(AXES, None, None),
        P(AXES, None),
        P(AXES, None, None),
        P(AXES, None, None),
    )
    return jax.shard_map(
        local,
        mesh=mesh,
        in_specs=placed,
        out_specs=(P(AXES, None, None), P(AXES, None, None)),
        check_vma=False,
    )
```

```python
import functools
import math

import jax
import jax.numpy as jnp
from jax import lax
from jax.experimental import pallas as pl
from jax.experimental.pallas import tpu as pltpu
from jax.sharding import PartitionSpec as P

SCALE_LENGTH = 0.5
NUGGET = 0.5
SQRT_THREE = math.sqrt(3.0)
LANES = 128
HIGHEST = lax.Precision.HIGHEST
F32 = jnp.float32
NN = (((1,), (0,)), ((), ()))
NT = (((1,), (1,)), ((), ()))
AXES = ("grp", "dev")
VMEM_LIMIT = 48 * 1024 * 1024
CLOSE = 2e-3
ALWAYS = 3
ROWS = 128


def split(value):
    high = value.astype(jnp.bfloat16)
    return high, (value - high.astype(F32)).astype(jnp.bfloat16)


def dot(left, right, dims=NN, precision=None):
    return lax.dot_general(left, right, dims, precision=precision, preferred_element_type=F32)


def split_fine(value):
    high = value.astype(jnp.bfloat16)
    rest = value - high.astype(F32)
    middle = rest.astype(jnp.bfloat16)
    return high, middle, (rest - middle.astype(F32)).astype(jnp.bfloat16)


def taken(base, left, right, dims=NN, rows=None):
    count = len(left)
    pieces = []
    rows = rows or base.shape[0]
    for first in range(0, base.shape[0], rows):
        total = base[first : first + rows]
        cut = [part[first : first + rows] for part in left]
        for at in range(count):
            group = None
            for other in range(count - 1 - at, -1, -1):
                term = dot(cut[other], right[at], dims)
                group = term if group is None else group + term
            total = total - group
        pieces.append(total)
    return pieces[0] if len(pieces) == 1 else jnp.concatenate(pieces, axis=0)


def newton_levels(order):
    least = 1.0 - CLOSE
    levels = [(1.0, 1.0 / least - NUGGET)]
    while levels[-1][1] < order + NUGGET:
        reached = least / (2.0 - least)
        least = 1.0 - math.sqrt(1.0 - reached)
        levels.append((2.0 / (1.0 + reached), 1.0 / least - NUGGET))
    return levels


def inverse(matrix, ahead, guess):
    order = matrix.shape[0]
    rows = lax.broadcasted_iota(jnp.int32, (order, order), 0)
    columns = lax.broadcasted_iota(jnp.int32, (order, order), 1)
    identity = (rows == columns).astype(F32)
    levels = newton_levels(order)
    always = min(ALWAYS, len(levels) - 1)
    bound = jnp.minimum(jnp.max(jnp.sum(jnp.abs(matrix), axis=0)), order + NUGGET)
    start = 2.0 / (NUGGET + levels[always][1])
    for level in range(always + 1, len(levels)):
        start = jnp.where(bound > levels[level - 1][1], 2.0 / (NUGGET + levels[level][1]), start)
    ahead[...] = start * matrix
    guess[...] = start * identity

    def advance(scale, now, held, only_guess=False):
        now_parts = split(now)
        new_held = scale * taken(2.0 * held, split(held), now_parts, rows=ROWS)
        return (None if only_guess else scale * taken(2.0 * now, now_parts, now_parts, rows=ROWS)), new_held

    for level in range(len(levels) - 1, always, -1):

        @pl.when(bound > levels[level - 1][1])
        def _(scale=levels[level][0]):
            ahead[...], guess[...] = advance(scale, ahead[...], guess[...])

    now, held = ahead[...], guess[...]
    for level in range(always, 0, -1):
        now, held = advance(levels[level][0], now, held, level == 1)
    error = taken(identity, split_fine(matrix), split_fine(held), rows=ROWS)
    return taken(held, split(held), split(-error), rows=ROWS)


def slot_list(slots):
    return [slot for slot in range(slots) if slot != 1]


def mirrored(index, size):
    bits = size.bit_length() - 1
    return sum(((index >> bit) & 1) << (bits - 1 - bit) for bit in range(bits))


def covariance(first, second, alive, same):
    points = second.shape[1]
    rows_at_once = 64
    parts = []
    for start in range(0, points, rows_at_once):
        down = first[start : start + rows_at_once]
        total = None
        for k in range(3):
            offset = down[:, k : k + 1] - second[k : k + 1, :]
            total = offset * offset if total is None else total + offset * offset
        scaled = jnp.sqrt(total)
        value = (1.0 + scaled) * jnp.exp(-scaled) * alive
        if same:
            row = lax.broadcasted_iota(jnp.int32, value.shape, 0) + start
            column = lax.broadcasted_iota(jnp.int32, value.shape, 1)
            value = value + jnp.where(row == column, NUGGET * alive + (1.0 - alive), 0.0)
        parts.append(value)
    return jnp.concatenate(parts, axis=0)


def half_place(index, me, coarse):
    return index ^ ((me & 1) * (coarse // 2))


def live_of(index):
    return (index >= 0).astype(F32)


def pack_kernel(sizes, locations, observed, noise, nbr, packed, noise_out, nbr_out, done):
    fields, points, coarse, slots = sizes
    pieces = points // LANES
    first = fields * pieces
    packed[first:] = jnp.zeros((4 * pieces, LANES), F32)
    copies = []
    for at in range(pieces):
        lanes = pl.ds(at * LANES, LANES)
        copies.append((observed.at[0, :, lanes], packed.at[pl.ds(at * fields, fields)]))
        copies.append((locations.at[0, :, lanes], packed.at[pl.ds(first + 4 * at, 3)]))
    copies += [(noise, noise_out), (nbr, nbr_out)]
    copies = [pltpu.make_async_copy(*copy, done.at[at]) for at, copy in enumerate(copies)]
    for copy in copies:
        copy.start()
    for copy in copies:
        copy.wait()


def fields_of(entry, fields, points):
    return jnp.concatenate([entry[at * fields : (at + 1) * fields] for at in range(points // LANES)], axis=1)


def places_of(entry, fields, points):
    pieces = points // LANES
    rows = [entry[fields * pieces + 4 * at :][:4] for at in range(pieces)]
    return jnp.concatenate(rows, axis=1) * (SQRT_THREE / SCALE_LENGTH)


def factor_kernel(sizes, nbr, me, before, table, mine, noise, part, back_out, last_out, columns, lower, ahead, guess):
    fields, points, coarse, slots = sizes
    used = slot_list(slots)
    own = len(used)
    ids = [nbr[0, slot] for slot in used] + [me[0]]
    here = lax.rem(me[0], coarse)
    entries = [before[0]]
    entries += [table[mirrored(jnp.maximum(index, 0) ^ here, coarse)] for index in ids[1:own]]
    entries += [mine[...]]
    live = [live_of(index) for index in ids]
    values = [fields_of(entry, fields, points) * alive for entry, alive in zip(entries, live)]
    places = [places_of(entry, fields, points) for entry in entries]
    turned = [jnp.transpose(jnp.concatenate([place, place], axis=0)) for place in places]

    def at(i, end=None):
        return pl.ds(i * points, ((i + 1 if end is None else end) - i) * points)

    for j in range(own + 1):
        for i in range(j, own + 1):
            columns[j, at(i)] = covariance(turned[i], places[j], live[i] * live[j], i == j)
    for k in range(own):
        middle = inverse(columns[k, at(k)], ahead, guess)
        side = columns[k, at(k + 1, own + 1)]
        below = -taken(jnp.zeros_like(side), split_fine(side), split_fine(middle))
        lower[k, at(k + 1, own + 1)] = below
        side_parts, below_parts = split(side), split(below)
        for j in range(k + 1, own + 1):
            cut = (j - k - 1) * points
            left = [piece[cut:] for piece in below_parts]
            right = [piece[cut : cut + points] for piece in side_parts]
            columns[j, at(j, own + 1)] = taken(columns[j, at(j, own + 1)], left, right, NT)
    for k in range(own - 1, -1, -1):
        total = lower[k, at(own)]
        if k + 1 < own:
            done = back_out[:, (k + 1) * points :]
            total = taken(total, split(done), split(lower[k, at(k + 1, own)]))
        back_out[:, k * points : (k + 1) * points] = total
    last = inverse(columns[own, at(own)], ahead, guess)
    last_out[...] = last
    back = {k: split(back_out[:, k * points : (k + 1) * points]) for k in range(own)}

    middle, spread, slot_parts = apply_block(values, back, split(last))
    own_part = spread + noise[0] * values[own]
    part[...] = jnp.zeros_like(part)
    product = jnp.sum(middle * spread + noise[0] * values[own] * values[own], axis=1, keepdims=True)
    square = jnp.sum(values[own] * values[own], axis=1, keepdims=True)
    part[coarse] = in_lanes([product, square], (fields, points))
    part[coarse + 1] = own_part
    part[coarse + 2] = slot_parts[0]
    for index, value in zip(ids, slot_parts + [own_part]):

        @pl.when((index >= 0) & (index < coarse))
        def _(index=index, value=value):
            place = half_place(index, me[0], coarse)
            part[place] = part[place] + value


def in_lanes(columns, shape):
    lane = lax.broadcasted_iota(jnp.int32, shape, 1)
    total = jnp.zeros(shape, F32)
    for at, column in enumerate(columns):
        total = jnp.where(lane == at, column, total)
    return total


def apply_block(values, back, last):
    own = len(values) - 1
    middle = values[own]
    for k in range(own):
        middle = taken(middle, split(values[k]), back[k], NT)
    spread = -taken(jnp.zeros_like(middle), split(middle), last)
    spread_parts = split(spread)
    slot_parts = [taken(jnp.zeros_like(middle), spread_parts, back[k]) for k in range(own)]
    return middle, spread, slot_parts


def step_kernel(
    sizes, nbr, me, before, table, mine, noise, part, rows, other_rows, scalars, near, far, back, last,
    sends, image_out, residual_out, ratio_out,
):
    fields, points, coarse, slots = sizes
    used = slot_list(slots)
    own = len(used)
    ids = [nbr[0, slot] for slot in used] + [me[0]]
    here = lax.rem(me[0], coarse)
    product = scalars[0, :, 0:1]
    norm_now = scalars[0, :, 1:2]
    alpha = norm_now / product
    half = coarse // 2
    even = (me[0] & 1) == 0
    values = []
    for at, index in enumerate(ids):
        place = half_place(jnp.clip(index, 0, coarse - 1), me[0], coarse)
        image = jnp.where(place < half, rows[place & (half - 1)], other_rows[place & (half - 1)])
        if at == 0:
            entry = before[0]
            image = jnp.where(index < coarse, image, jnp.where(even, far[0], near[0]) + part[coarse + 2])
        elif at == own:
            entry = mine[...]
            image = jnp.where(index < coarse, image, part[coarse + 1] + jnp.where(even, near[0], far[0]))
        else:
            entry = table[mirrored(jnp.maximum(index, 0) ^ here, coarse)]
        values.append((fields_of(entry, fields, points) - alpha * image) * live_of(index))
    back_parts = {k: split(back[:, k * points : (k + 1) * points]) for k in range(own)}
    middle, spread, slot_parts = apply_block(values, back_parts, split(last[...]))
    residual = values[own]
    inner = jnp.sum(middle * spread + noise[0] * residual * residual, axis=1, keepdims=True)
    cross = jnp.sum(residual * image, axis=1, keepdims=True)
    square = jnp.sum(residual * residual, axis=1, keepdims=True)
    sends[...] = jnp.zeros_like(sends)
    sends[coarse] = in_lanes([inner, cross, square], (fields, points))
    sends[coarse + 1] = slot_parts[0]
    for index, value in zip(ids[1:own], slot_parts[1:]):

        @pl.when(index >= 0)
        def _(index=index, value=value):
            place = mirrored(index ^ here, coarse)
            sends[place] = sends[place] + value

    image_out[0] = image
    image_out[1] = spread + noise[0] * residual
    residual_out[...] = residual
    ratio_out[...] = in_lanes([alpha, norm_now, product], (fields, LANES))


def finish_kernel(sizes, me, received, shifted, images, residual, ratios, mine, solution_out, residual_out):
    fields, points, coarse, slots = sizes
    owner = (me[0] < coarse).astype(F32)
    spread = images[1] + shifted[0] + owner * received[0]
    scalars = received[1]
    alpha, norm_first, product_first = ratios[:, 0:1], ratios[:, 1:2], ratios[:, 2:3]
    inner, cross, norm_now = scalars[:, 0:1], scalars[:, 1:2], scalars[:, 2:3]
    beta = norm_now / norm_first
    product = inner + beta * (2.0 * cross + beta * product_first)
    step = norm_now / product
    observed = fields_of(mine[...], fields, points)
    direction = residual[...] + beta * observed
    solution_out[0] = alpha * observed + step * direction
    residual_out[0] = residual[...] - step * (spread + beta * images[0])


def call(kernel, sizes, outs, in_spaces, scratch=()):
    return pl.pallas_call(
        functools.partial(kernel, sizes),
        out_shape=[out if hasattr(out, "dtype") else jax.ShapeDtypeStruct(out, F32) for out in outs],
        in_specs=[pl.BlockSpec(memory_space=space) for space in in_spaces],
        out_specs=[pl.BlockSpec(memory_space=pltpu.VMEM)] * len(outs),
        scratch_shapes=list(scratch),
        compiler_params=pltpu.CompilerParams(vmem_limit_bytes=VMEM_LIMIT),
    )


def powers(size):
    assert size & (size - 1) == 0
    return [1 << bit for bit in range(size.bit_length() - 1)]


def swapped(value, axis, reach):
    return lax.ppermute(value, axis, [(at, at ^ reach) for at in range(lax.axis_size(axis))])


def exchanges():
    steps, bit = [], 0
    for axis in AXES[::-1]:
        for reach in powers(lax.axis_size(axis)):
            steps.append((axis, reach, bit))
            bit += 1
    return steps


def carry(shifted, ends, got, number, bit, down):
    full = (1 << bit) - 1
    low, upper = number & full, ((number >> bit) & 1) == 1
    takes = jnp.where(down, ~upper & (low == full), upper & (low == 0))
    return jnp.where(takes, got, shifted), jnp.where(upper ^ down, ends, got)


def local(locations, neighbours, observations, noise_prec):
    blocks, _, points = locations.shape
    fields = observations.shape[1]
    slots = neighbours.shape[1]
    assert blocks == 1
    coarse = lax.axis_size("dev")
    sizes = (fields, points, coarse, slots)
    depth = len(slot_list(slots)) * points
    pieces = points // LANES
    me = lax.axis_index(AXES).astype(jnp.int32)
    group = lax.axis_index("grp")
    smem, vmem = pltpu.SMEM, pltpu.VMEM
    square, tile = (points, points), (fields, points)
    steps = exchanges()

    mine, noise, nbr = call(
        pack_kernel,
        sizes,
        [((fields + 4) * pieces, LANES), noise_prec, neighbours],
        [pl.ANY] * 4,
        [pltpu.SemaphoreType.DMA((2 * pieces + 2,))],
    )(locations, observations, noise_prec, neighbours)
    before, table = mine[None], mine[None]
    for axis, reach, bit in steps[::-1]:
        got = swapped(jnp.concatenate([table, before], axis=0), axis, reach)
        low = (1 << bit) - 1
        before = jnp.where((me & low) == low, got[-1:], before)
        if axis == "grp":
            table = jnp.where((group & reach) != 0, got[:-1], table)
        else:
            table = jnp.concatenate([table, got[:-1]], axis=0)
    at = me.reshape(1)
    part, back, last = call(
        factor_kernel,
        sizes,
        [(coarse + 3,) + tile, (points, depth), square],
        [smem, smem] + [vmem] * 4,
        [pltpu.VMEM((slots, slots * points, points), F32)] * 2 + [pltpu.VMEM(square, F32)] * 2,
    )(nbr, at, before, table, mine, noise)

    half, odd = coarse // 2, (me & 1) == 1
    got = swapped(part[half:], "dev", 1)
    rows, scalars = part[:half] + got[:half], part[coarse : coarse + 1] + got[half : half + 1]
    up, down = got[half + 1 : half + 2], got[half + 2 :]
    near, ends, far = jnp.where(odd, up, down), jnp.where(odd, down, up), jnp.zeros_like(up)
    for axis, reach, bit in steps[1:]:
        got = swapped(jnp.concatenate([rows, scalars, ends], axis=0), axis, reach)
        rows, scalars = rows + got[:half], scalars + got[half : half + 1]
        far, ends = carry(far, ends, got[half + 1 :], me >> 1, bit - 1, odd)
    other_rows = swapped(rows, "dev", 1)
    sends, images, residual, ratios = call(
        step_kernel,
        sizes,
        [(coarse + 2,) + tile, (2,) + tile, tile, (fields, LANES)],
        [smem, smem] + [vmem] * 12,
    )(nbr, at, before, table, mine, noise, part, rows, other_rows, scalars, near, far, back, last)

    summed, ends, shifted = sends[:-1], sends[-1:], jnp.zeros_like(sends[-1:])
    for axis, reach, bit in steps:
        kept = (summed.shape[0] - 1) // 2 if axis == "dev" else 0
        got = swapped(jnp.concatenate([summed[kept:], ends], axis=0), axis, reach)
        if axis == "dev":
            summed = jnp.concatenate([summed[:kept], summed[-1:]], axis=0)
        summed = summed + got[:-1]
        shifted, ends = carry(shifted, ends, got[-1:], me, bit, True)
    return tuple(
        call(finish_kernel, sizes, [observations.shape] * 2, [smem] + [vmem] * 6)(
            at, summed, shifted, images, residual, ratios, mine
        )
    )


def solution(mesh):
    placed = (
        P(AXES, None, None),
        P(AXES, None),
        P(AXES, None, None),
        P(AXES, None, None),
    )
    return jax.shard_map(
        local,
        mesh=mesh,
        in_specs=placed,
        out_specs=(P(AXES, None, None), P(AXES, None, None)),
        check_vma=False,
    )
```

```python
import functools
import math

import jax
import jax.numpy as jnp
from jax import lax
from jax.experimental import pallas as pl
from jax.experimental.pallas import tpu as pltpu
from jax.sharding import PartitionSpec as P

SCALE_LENGTH = 0.5
NUGGET = 0.5
SQRT_THREE = math.sqrt(3.0)
LANES = 128
HIGHEST = lax.Precision.HIGHEST
F32 = jnp.float32
NN = (((1,), (0,)), ((), ()))
NT = (((1,), (1,)), ((), ()))
AXES = ("grp", "dev")
VMEM_LIMIT = 48 * 1024 * 1024
CLOSE = 2e-3
ROWS = 128


def split(value):
    high = value.astype(jnp.bfloat16)
    return high, (value - high.astype(F32)).astype(jnp.bfloat16)


def dot(left, right, dims=NN, precision=None):
    return lax.dot_general(left, right, dims, precision=precision, preferred_element_type=F32)


def split_fine(value):
    high = value.astype(jnp.bfloat16)
    rest = value - high.astype(F32)
    middle = rest.astype(jnp.bfloat16)
    return high, middle, (rest - middle.astype(F32)).astype(jnp.bfloat16)


def taken(base, left, right, dims=NN, rows=None):
    count = len(left)
    pieces = []
    rows = rows or base.shape[0]
    for first in range(0, base.shape[0], rows):
        total = base[first : first + rows]
        cut = [part[first : first + rows] for part in left]
        for at in range(count):
            group = None
            for other in range(count - 1 - at, -1, -1):
                term = dot(cut[other], right[at], dims)
                group = term if group is None else group + term
            total = total - group
        pieces.append(total)
    return pieces[0] if len(pieces) == 1 else jnp.concatenate(pieces, axis=0)


def newton_levels(order):
    least = 1.0 - CLOSE
    levels = [(1.0, 1.0 / least - NUGGET)]
    while levels[-1][1] < order + NUGGET:
        reached = least / (2.0 - least)
        least = 1.0 - math.sqrt(1.0 - reached)
        levels.append((2.0 / (1.0 + reached), 1.0 / least - NUGGET))
    return levels


def inverse(matrix, ahead, guess, always, beside=()):
    order = matrix.shape[0]
    rows = lax.broadcasted_iota(jnp.int32, (order, order), 0)
    columns = lax.broadcasted_iota(jnp.int32, (order, order), 1)
    identity = (rows == columns).astype(F32)
    levels = newton_levels(order)
    always = min(always, len(levels) - 1)
    bound = jnp.minimum(jnp.max(jnp.sum(jnp.abs(matrix), axis=0)), order + NUGGET)
    start = 2.0 / (NUGGET + levels[always][1])
    for level in range(always + 1, len(levels)):
        start = jnp.where(bound > levels[level - 1][1], 2.0 / (NUGGET + levels[level][1]), start)
    ahead[...] = start * matrix
    guess[...] = start * identity

    def advance(scale, now, held, only_guess=False):
        now_parts = split(now)
        new_now = None if only_guess else scale * taken(2.0 * now, now_parts, now_parts, rows=ROWS)
        new_held = scale * taken(2.0 * held, split(held), now_parts, rows=ROWS)
        return new_now, new_held

    for level in range(len(levels) - 1, always, -1):

        @pl.when(bound > levels[level - 1][1])
        def _(scale=levels[level][0]):
            ahead[...], guess[...] = advance(scale, ahead[...], guess[...])

    beside = list(beside)

    def also(left):
        while len(beside) > left:
            beside.pop(0)()

    count = len(beside)
    for level in range(always, 1, -1):
        ahead[...], guess[...] = advance(levels[level][0], ahead[...], guess[...])
        also(count * level // (always + 1))
    guess[...] = advance(levels[1][0], ahead[...], guess[...], True)[1]
    also(count // (always + 1))
    held = guess[...]
    ahead[...] = -taken(identity, split_fine(matrix), split_fine(held), rows=ROWS)
    also(0)
    held = guess[...]
    guess[...] = taken(held, split(held), split(ahead[...]), rows=ROWS)
    return guess[...]


def slot_list(slots):
    return [slot for slot in range(slots) if slot != 1]


def mirrored(index, size):
    bits = size.bit_length() - 1
    return sum(((index >> bit) & 1) << (bits - 1 - bit) for bit in range(bits))


def covariance(first, second, alive, same):
    points = second.shape[1]
    rows_at_once = 64
    parts = []
    for start in range(0, points, rows_at_once):
        down = first[start : start + rows_at_once]
        total = None
        for k in range(3):
            offset = down[:, k : k + 1] - second[k : k + 1, :]
            total = offset * offset if total is None else total + offset * offset
        scaled = jnp.sqrt(total)
        value = (1.0 + scaled) * jnp.exp(-scaled) * alive
        if same:
            row = lax.broadcasted_iota(jnp.int32, value.shape, 0) + start
            column = lax.broadcasted_iota(jnp.int32, value.shape, 1)
            value = value + jnp.where(row == column, NUGGET * alive + (1.0 - alive), 0.0)
        parts.append(value)
    return jnp.concatenate(parts, axis=0)


def half_place(index, me, coarse):
    return index ^ ((me & 1) * (coarse // 2))


def live_of(index):
    return (index >= 0).astype(F32)


def pack_kernel(sizes, locations, observed, noise, nbr, packed, noise_out, nbr_out, done):
    fields, points, coarse, slots = sizes
    pieces = points // LANES
    first = fields * pieces
    packed[first:] = jnp.zeros((4 * pieces, LANES), F32)
    copies = []
    for at in range(pieces):
        lanes = pl.ds(at * LANES, LANES)
        copies.append((observed.at[0, :, lanes], packed.at[pl.ds(at * fields, fields)]))
        copies.append((locations.at[0, :, lanes], packed.at[pl.ds(first + 4 * at, 3)]))
    copies += [(noise, noise_out), (nbr, nbr_out)]
    copies = [pltpu.make_async_copy(*copy, done.at[at]) for at, copy in enumerate(copies)]
    for copy in copies:
        copy.start()
    for copy in copies:
        copy.wait()


def fields_of(entry, fields, points):
    return jnp.concatenate([entry[at * fields : (at + 1) * fields] for at in range(points // LANES)], axis=1)


def places_of(entry, fields, points):
    pieces = points // LANES
    rows = [entry[fields * pieces + 4 * at :][:4] for at in range(pieces)]
    return jnp.concatenate(rows, axis=1) * (SQRT_THREE / SCALE_LENGTH)


def factor_kernel(sizes, nbr, me, before, table, mine, noise, part, back_out, last_out, columns, lower, ahead, guess):
    fields, points, coarse, slots = sizes
    used = slot_list(slots)
    own = len(used)
    ids = [nbr[0, slot] for slot in used] + [me[0]]
    here = lax.rem(me[0], coarse)
    entries = [before[0]]
    entries += [table[mirrored(jnp.maximum(index, 0) ^ here, coarse)] for index in ids[1:own]]
    entries += [mine[...]]
    live = [live_of(index) for index in ids]
    values = [fields_of(entry, fields, points) * alive for entry, alive in zip(entries, live)]
    places = [places_of(entry, fields, points) for entry in entries]
    turned = [jnp.transpose(jnp.concatenate([place, place], axis=0)) for place in places]

    def at(i, end=None):
        return pl.ds(i * points, ((i + 1 if end is None else end) - i) * points)

    def build(i, j):
        columns[j, at(i)] = covariance(turned[i], places[j], live[i] * live[j], i == j)

    build(0, 0)
    later = [functools.partial(build, i, j) for j in range(own + 1) for i in range(max(j, 1), own + 1)]
    for k in range(own):
        middle = inverse(columns[k, at(k)], ahead, guess, 6 if k == 0 else 3, later if k == 0 else ())
        side = columns[k, at(k + 1, own + 1)]
        below = -taken(jnp.zeros_like(side), split_fine(side), split_fine(middle))
        lower[k, at(k + 1, own + 1)] = below
        side_parts, below_parts = split(side), split(below)
        for j in range(k + 1, own + 1):
            cut = (j - k - 1) * points
            left = [piece[cut:] for piece in below_parts]
            right = [piece[cut : cut + points] for piece in side_parts]
            columns[j, at(j, own + 1)] = taken(columns[j, at(j, own + 1)], left, right, NT)
    def go_back(k):
        total = lower[k, at(own)]
        if k + 1 < own:
            done = back_out[:, (k + 1) * points :]
            total = taken(total, split(done), split(lower[k, at(k + 1, own)]))
        back_out[:, k * points : (k + 1) * points] = total

    last = inverse(columns[own, at(own)], ahead, guess, 3, [functools.partial(go_back, k) for k in range(own - 1, -1, -1)])
    last_out[...] = last
    back = {k: split(back_out[:, k * points : (k + 1) * points]) for k in range(own)}

    middle, spread, slot_parts = apply_block(values, back, split(last))
    own_part = spread + noise[0] * values[own]
    part[...] = jnp.zeros_like(part)
    product = jnp.sum(middle * spread + noise[0] * values[own] * values[own], axis=1, keepdims=True)
    square = jnp.sum(values[own] * values[own], axis=1, keepdims=True)
    part[coarse] = in_lanes([product, square], (fields, points))
    part[coarse + 1] = own_part
    part[coarse + 2] = slot_parts[0]
    for index, value in zip(ids, slot_parts + [own_part]):

        @pl.when((index >= 0) & (index < coarse))
        def _(index=index, value=value):
            place = half_place(index, me[0], coarse)
            part[place] = part[place] + value


def in_lanes(columns, shape):
    lane = lax.broadcasted_iota(jnp.int32, shape, 1)
    total = jnp.zeros(shape, F32)
    for at, column in enumerate(columns):
        total = jnp.where(lane == at, column, total)
    return total


def apply_block(values, back, last):
    own = len(values) - 1
    middle = values[own]
    for k in range(own):
        middle = taken(middle, split(values[k]), back[k], NT)
    spread = -taken(jnp.zeros_like(middle), split(middle), last)
    spread_parts = split(spread)
    slot_parts = [taken(jnp.zeros_like(middle), spread_parts, back[k]) for k in range(own)]
    return middle, spread, slot_parts


def step_kernel(
    sizes, nbr, me, before, table, mine, noise, part, rows, other_rows, scalars, near, far, back, last,
    sends, image_out, residual_out, ratio_out,
):
    fields, points, coarse, slots = sizes
    used = slot_list(slots)
    own = len(used)
    ids = [nbr[0, slot] for slot in used] + [me[0]]
    here = lax.rem(me[0], coarse)
    product = scalars[0, :, 0:1]
    norm_now = scalars[0, :, 1:2]
    alpha = norm_now / product
    half = coarse // 2
    even = (me[0] & 1) == 0
    values = []
    for at, index in enumerate(ids):
        place = half_place(jnp.clip(index, 0, coarse - 1), me[0], coarse)
        image = jnp.where(place < half, rows[place & (half - 1)], other_rows[place & (half - 1)])
        if at == 0:
            entry = before[0]
            image = jnp.where(index < coarse, image, jnp.where(even, far[0], near[0]) + part[coarse + 2])
        elif at == own:
            entry = mine[...]
            image = jnp.where(index < coarse, image, part[coarse + 1] + jnp.where(even, near[0], far[0]))
        else:
            entry = table[mirrored(jnp.maximum(index, 0) ^ here, coarse)]
        values.append((fields_of(entry, fields, points) - alpha * image) * live_of(index))
    back_parts = {k: split(back[:, k * points : (k + 1) * points]) for k in range(own)}
    middle, spread, slot_parts = apply_block(values, back_parts, split(last[...]))
    residual = values[own]
    inner = jnp.sum(middle * spread + noise[0] * residual * residual, axis=1, keepdims=True)
    cross = jnp.sum(residual * image, axis=1, keepdims=True)
    square = jnp.sum(residual * residual, axis=1, keepdims=True)
    sends[...] = jnp.zeros_like(sends)
    sends[coarse] = in_lanes([inner, cross, square], (fields, points))
    sends[coarse + 1] = slot_parts[0]
    for index, value in zip(ids[1:own], slot_parts[1:]):

        @pl.when(index >= 0)
        def _(index=index, value=value):
            place = mirrored(index ^ here, coarse)
            sends[place] = sends[place] + value

    image_out[0] = image
    image_out[1] = spread + noise[0] * residual
    residual_out[...] = residual
    ratio_out[...] = in_lanes([alpha, norm_now, product], (fields, LANES))


def finish_kernel(sizes, me, received, shifted, images, residual, ratios, mine, solution_out, residual_out):
    fields, points, coarse, slots = sizes
    owner = (me[0] < coarse).astype(F32)
    spread = images[1] + shifted[0] + owner * received[0]
    scalars = received[1]
    alpha, norm_first, product_first = ratios[:, 0:1], ratios[:, 1:2], ratios[:, 2:3]
    inner, cross, norm_now = scalars[:, 0:1], scalars[:, 1:2], scalars[:, 2:3]
    beta = norm_now / norm_first
    product = inner + beta * (2.0 * cross + beta * product_first)
    step = norm_now / product
    observed = fields_of(mine[...], fields, points)
    direction = residual[...] + beta * observed
    solution_out[0] = alpha * observed + step * direction
    residual_out[0] = residual[...] - step * (spread + beta * images[0])


def call(kernel, sizes, outs, in_spaces, scratch=()):
    return pl.pallas_call(
        functools.partial(kernel, sizes),
        out_shape=[out if hasattr(out, "dtype") else jax.ShapeDtypeStruct(out, F32) for out in outs],
        in_specs=[pl.BlockSpec(memory_space=space) for space in in_spaces],
        out_specs=[pl.BlockSpec(memory_space=pltpu.VMEM)] * len(outs),
        scratch_shapes=list(scratch),
        compiler_params=pltpu.CompilerParams(vmem_limit_bytes=VMEM_LIMIT),
    )


def powers(size):
    assert size & (size - 1) == 0
    return [1 << bit for bit in range(size.bit_length() - 1)]


def swapped(value, axis, reach):
    return lax.ppermute(value, axis, [(at, at ^ reach) for at in range(lax.axis_size(axis))])


def exchanges():
    steps, bit = [], 0
    for axis in AXES[::-1]:
        for reach in powers(lax.axis_size(axis)):
            steps.append((axis, reach, bit))
            bit += 1
    return steps


def carry(shifted, ends, got, number, bit, down):
    full = (1 << bit) - 1
    low, upper = number & full, ((number >> bit) & 1) == 1
    takes = jnp.where(down, ~upper & (low == full), upper & (low == 0))
    return jnp.where(takes, got, shifted), jnp.where(upper ^ down, ends, got)


def local(locations, neighbours, observations, noise_prec):
    blocks, _, points = locations.shape
    fields = observations.shape[1]
    slots = neighbours.shape[1]
    assert blocks == 1
    coarse = lax.axis_size("dev")
    sizes = (fields, points, coarse, slots)
    depth = len(slot_list(slots)) * points
    pieces = points // LANES
    me = lax.axis_index(AXES).astype(jnp.int32)
    group = lax.axis_index("grp")
    smem, vmem = pltpu.SMEM, pltpu.VMEM
    square, tile = (points, points), (fields, points)
    steps = exchanges()

    mine, noise, nbr = call(
        pack_kernel,
        sizes,
        [((fields + 4) * pieces, LANES), noise_prec, neighbours],
        [pltpu.HBM] * 4,
        [pltpu.SemaphoreType.DMA((2 * pieces + 2,))],
    )(locations, observations, noise_prec, neighbours)
    before, table = mine[None], mine[None]
    for axis, reach, bit in steps[::-1]:
        got = swapped(jnp.concatenate([table, before], axis=0), axis, reach)
        low = (1 << bit) - 1
        before = jnp.where((me & low) == low, got[-1:], before)
        if axis == "grp":
            table = jnp.where((group & reach) != 0, got[:-1], table)
        else:
            table = jnp.concatenate([table, got[:-1]], axis=0)
    at = me.reshape(1)
    part, back, last = call(
        factor_kernel,
        sizes,
        [(coarse + 3,) + tile, (points, depth), square],
        [smem, smem] + [vmem] * 4,
        [pltpu.VMEM((slots, slots * points, points), F32)] * 2 + [pltpu.VMEM(square, F32)] * 2,
    )(nbr, at, before, table, mine, noise)

    half, odd = coarse // 2, (me & 1) == 1
    got = swapped(part[half:], "dev", 1)
    rows, scalars = part[:half] + got[:half], part[coarse : coarse + 1] + got[half : half + 1]
    up, down = got[half + 1 : half + 2], got[half + 2 :]
    near, ends, far = jnp.where(odd, up, down), jnp.where(odd, down, up), jnp.zeros_like(up)
    for axis, reach, bit in steps[1:]:
        got = swapped(jnp.concatenate([rows, scalars, ends], axis=0), axis, reach)
        rows, scalars = rows + got[:half], scalars + got[half : half + 1]
        far, ends = carry(far, ends, got[half + 1 :], me >> 1, bit - 1, odd)
    other_rows = swapped(rows, "dev", 1)
    sends, images, residual, ratios = call(
        step_kernel,
        sizes,
        [(coarse + 2,) + tile, (2,) + tile, tile, (fields, LANES)],
        [smem, smem] + [vmem] * 12,
    )(nbr, at, before, table, mine, noise, part, rows, other_rows, scalars, near, far, back, last)

    summed, ends, shifted = sends[:-1], sends[-1:], jnp.zeros_like(sends[-1:])
    for axis, reach, bit in steps:
        kept = (summed.shape[0] - 1) // 2 if axis == "dev" else 0
        got = swapped(jnp.concatenate([summed[kept:], ends], axis=0), axis, reach)
        if axis == "dev":
            summed = jnp.concatenate([summed[:kept], summed[-1:]], axis=0)
        summed = summed + got[:-1]
        shifted, ends = carry(shifted, ends, got[-1:], me, bit, True)
    return tuple(
        call(finish_kernel, sizes, [observations.shape] * 2, [smem] + [vmem] * 6)(
            at, summed, shifted, images, residual, ratios, mine
        )
    )


def solution(mesh):
    placed = (
        P(AXES, None, None),
        P(AXES, None),
        P(AXES, None, None),
        P(AXES, None, None),
    )
    return jax.shard_map(
        local,
        mesh=mesh,
        in_specs=placed,
        out_specs=(P(AXES, None, None), P(AXES, None, None)),
        check_vma=False,
    )
```

```python
import functools
import math

import jax
import jax.numpy as jnp
from jax import lax
from jax.experimental import pallas as pl
from jax.experimental.pallas import tpu as pltpu
from jax.sharding import PartitionSpec as P

SCALE_LENGTH = 0.5
NUGGET = 0.5
SQRT_THREE = math.sqrt(3.0)
LANES = 128
HIGHEST = lax.Precision.HIGHEST
F32 = jnp.float32
NN = (((1,), (0,)), ((), ()))
NT = (((1,), (1,)), ((), ()))
AXES = ("grp", "dev")
VMEM_LIMIT = 48 * 1024 * 1024
CLOSE = 2e-3
ROWS = 128
TOPS = (3, 4, 6)


def split(value):
    high = value.astype(jnp.bfloat16)
    return high, (value - high.astype(F32)).astype(jnp.bfloat16)


def dot(left, right, dims=NN, precision=None):
    return lax.dot_general(left, right, dims, precision=precision, preferred_element_type=F32)


def split_fine(value):
    high = value.astype(jnp.bfloat16)
    rest = value - high.astype(F32)
    middle = rest.astype(jnp.bfloat16)
    return high, middle, (rest - middle.astype(F32)).astype(jnp.bfloat16)


def taken(base, left, right, dims=NN, rows=None):
    count = len(left)
    pieces = []
    rows = rows or base.shape[0]
    for first in range(0, base.shape[0], rows):
        total = base[first : first + rows]
        cut = [part[first : first + rows] for part in left]
        for at in range(count):
            group = None
            for other in range(count - 1 - at, -1, -1):
                term = dot(cut[other], right[at], dims)
                group = term if group is None else group + term
            total = total - group
        pieces.append(total)
    return pieces[0] if len(pieces) == 1 else jnp.concatenate(pieces, axis=0)


def newton_levels(order):
    least = 1.0 - CLOSE
    levels = [(1.0, 1.0 / least - NUGGET)]
    while levels[-1][1] < order + NUGGET:
        reached = least / (2.0 - least)
        least = 1.0 - math.sqrt(1.0 - reached)
        levels.append((2.0 / (1.0 + reached), 1.0 / least - NUGGET))
    return levels


def inverse(matrix, ahead, guess, beside=()):
    order = matrix.shape[0]
    rows = lax.broadcasted_iota(jnp.int32, (order, order), 0)
    columns = lax.broadcasted_iota(jnp.int32, (order, order), 1)
    identity = (rows == columns).astype(F32)
    levels = newton_levels(order)
    last = len(levels) - 1
    tops = [top for top in TOPS if top < last] + [last]
    tops += [] if len(tops) > 1 else [last]
    bound = jnp.minimum(jnp.max(jnp.sum(jnp.abs(matrix), axis=0)), order + NUGGET)
    start = 2.0 / (NUGGET + levels[tops[0]][1])
    for below, top in zip(tops, tops[1:]):
        start = jnp.where(bound > levels[below][1], 2.0 / (NUGGET + levels[top][1]), start)
    ahead[...] = start * matrix
    guess[...] = start * identity

    def advance(scale, now, held, only_guess=False):
        now_parts = split(now)
        new_now = None if only_guess else scale * taken(2.0 * now, now_parts, now_parts, rows=ROWS)
        new_held = scale * taken(2.0 * held, split(held), now_parts, rows=ROWS)
        return new_now, new_held

    for below, top in list(zip(tops, tops[1:]))[::-1]:

        @pl.when(bound > levels[below][1])
        def _(below=below, top=top):
            for level in range(top, below, -1):
                ahead[...], guess[...] = advance(levels[level][0], ahead[...], guess[...])

    always = tops[0]
    beside = list(beside)

    def also(left):
        while len(beside) > left:
            beside.pop(0)()

    count = len(beside)
    for level in range(always, 1, -1):
        ahead[...], guess[...] = advance(levels[level][0], ahead[...], guess[...])
        also(count * level // (always + 1))
    guess[...] = advance(levels[1][0], ahead[...], guess[...], True)[1]
    also(count // (always + 1))
    held = guess[...]
    ahead[...] = -taken(identity, split_fine(matrix), split_fine(held), rows=ROWS)
    also(0)
    held = guess[...]
    guess[...] = taken(held, split(held), split(ahead[...]), rows=ROWS)
    return guess[...]


def slot_list(slots):
    return [slot for slot in range(slots) if slot != 1]


def mirrored(index, size):
    bits = size.bit_length() - 1
    return sum(((index >> bit) & 1) << (bits - 1 - bit) for bit in range(bits))


def covariance(first, second, alive, same):
    points = second.shape[1]
    rows_at_once = 64
    parts = []
    for start in range(0, points, rows_at_once):
        down = first[start : start + rows_at_once]
        total = None
        for k in range(3):
            offset = down[:, k : k + 1] - second[k : k + 1, :]
            total = offset * offset if total is None else total + offset * offset
        scaled = jnp.sqrt(total)
        value = (1.0 + scaled) * jnp.exp(-scaled) * alive
        if same:
            row = lax.broadcasted_iota(jnp.int32, value.shape, 0) + start
            column = lax.broadcasted_iota(jnp.int32, value.shape, 1)
            value = value + jnp.where(row == column, NUGGET * alive + (1.0 - alive), 0.0)
        parts.append(value)
    return jnp.concatenate(parts, axis=0)


def half_place(index, me, coarse):
    return index ^ ((me & 1) * (coarse // 2))


def live_of(index):
    return (index >= 0).astype(F32)


def fields_of(entry, fields, points):
    return jnp.concatenate([entry[at * fields : (at + 1) * fields] for at in range(points // LANES)], axis=1)


def places_of(entry, fields, points):
    pieces = points // LANES
    rows = [entry[fields * pieces + 4 * at :][:4] for at in range(pieces)]
    return jnp.concatenate(rows, axis=1) * (SQRT_THREE / SCALE_LENGTH)


def factor_kernel(sizes, nbr, me, before, table, mine, noise, part, back_out, last_out, columns, lower, ahead, guess):
    fields, points, coarse, slots = sizes
    used = slot_list(slots)
    own = len(used)
    ids = [nbr[0, slot] for slot in used] + [me[0]]
    here = lax.rem(me[0], coarse)
    entries = [before[0]]
    entries += [table[mirrored(jnp.maximum(index, 0) ^ here, coarse)] for index in ids[1:own]]
    entries += [mine[...]]
    live = [live_of(index) for index in ids]
    values = [fields_of(entry, fields, points) * alive for entry, alive in zip(entries, live)]
    places = [places_of(entry, fields, points) for entry in entries]
    turned = [jnp.transpose(jnp.concatenate([place, place], axis=0)) for place in places]

    def at(i, end=None):
        return pl.ds(i * points, ((i + 1 if end is None else end) - i) * points)

    def build(i, j):
        columns[j, at(i)] = covariance(turned[i], places[j], live[i] * live[j], i == j)

    build(0, 0)
    later = [functools.partial(build, i, j) for j in range(own + 1) for i in range(max(j, 1), own + 1)]
    for k in range(own):
        middle = inverse(columns[k, at(k)], ahead, guess, later if k == 0 else ())
        side = columns[k, at(k + 1, own + 1)]
        below = -taken(jnp.zeros_like(side), split_fine(side), split_fine(middle))
        lower[k, at(k + 1, own + 1)] = below
        side_parts, below_parts = split(side), split(below)
        for j in range(k + 1, own + 1):
            cut = (j - k - 1) * points
            left = [piece[cut:] for piece in below_parts]
            right = [piece[cut : cut + points] for piece in side_parts]
            columns[j, at(j, own + 1)] = taken(columns[j, at(j, own + 1)], left, right, NT)
    def go_back(k):
        total = lower[k, at(own)]
        if k + 1 < own:
            done = back_out[:, (k + 1) * points :]
            total = taken(total, split(done), split(lower[k, at(k + 1, own)]))
        back_out[:, k * points : (k + 1) * points] = total

    last = inverse(columns[own, at(own)], ahead, guess, [functools.partial(go_back, k) for k in range(own - 1, -1, -1)])
    last_out[...] = last
    back = {k: split(back_out[:, k * points : (k + 1) * points]) for k in range(own)}

    middle, spread, slot_parts = apply_block(values, back, split(last))
    own_part = spread + noise[0] * values[own]
    part[...] = jnp.zeros_like(part)
    product = jnp.sum(middle * spread + noise[0] * values[own] * values[own], axis=1, keepdims=True)
    square = jnp.sum(values[own] * values[own], axis=1, keepdims=True)
    part[coarse] = in_lanes([product, square], (fields, points))
    part[coarse + 1] = own_part
    part[coarse + 2] = slot_parts[0]
    for index, value in zip(ids, slot_parts + [own_part]):

        @pl.when((index >= 0) & (index < coarse))
        def _(index=index, value=value):
            place = half_place(index, me[0], coarse)
            part[place] = part[place] + value


def in_lanes(columns, shape):
    lane = lax.broadcasted_iota(jnp.int32, shape, 1)
    total = jnp.zeros(shape, F32)
    for at, column in enumerate(columns):
        total = jnp.where(lane == at, column, total)
    return total


def apply_block(values, back, last):
    own = len(values) - 1
    middle = values[own]
    for k in range(own):
        middle = taken(middle, split(values[k]), back[k], NT)
    spread = -taken(jnp.zeros_like(middle), split(middle), last)
    spread_parts = split(spread)
    slot_parts = [taken(jnp.zeros_like(middle), spread_parts, back[k]) for k in range(own)]
    return middle, spread, slot_parts


def step_kernel(
    sizes, nbr, me, before, table, mine, noise, part, rows, other_rows, scalars, near, far, back, last,
    sends, image_out, residual_out, ratio_out,
):
    fields, points, coarse, slots = sizes
    used = slot_list(slots)
    own = len(used)
    ids = [nbr[0, slot] for slot in used] + [me[0]]
    here = lax.rem(me[0], coarse)
    product = scalars[0, :, 0:1]
    norm_now = scalars[0, :, 1:2]
    alpha = norm_now / product
    half = coarse // 2
    even = (me[0] & 1) == 0
    values = []
    for at, index in enumerate(ids):
        place = half_place(jnp.clip(index, 0, coarse - 1), me[0], coarse)
        image = jnp.where(place < half, rows[place & (half - 1)], other_rows[place & (half - 1)])
        if at == 0:
            entry = before[0]
            image = jnp.where(index < coarse, image, jnp.where(even, far[0], near[0]) + part[coarse + 2])
        elif at == own:
            entry = mine[...]
            image = jnp.where(index < coarse, image, part[coarse + 1] + jnp.where(even, near[0], far[0]))
        else:
            entry = table[mirrored(jnp.maximum(index, 0) ^ here, coarse)]
        values.append((fields_of(entry, fields, points) - alpha * image) * live_of(index))
    back_parts = {k: split(back[:, k * points : (k + 1) * points]) for k in range(own)}
    middle, spread, slot_parts = apply_block(values, back_parts, split(last[...]))
    residual = values[own]
    inner = jnp.sum(middle * spread + noise[0] * residual * residual, axis=1, keepdims=True)
    cross = jnp.sum(residual * image, axis=1, keepdims=True)
    square = jnp.sum(residual * residual, axis=1, keepdims=True)
    sends[...] = jnp.zeros_like(sends)
    sends[coarse] = in_lanes([inner, cross, square], (fields, points))
    sends[coarse + 1] = slot_parts[0]
    for index, value in zip(ids[1:own], slot_parts[1:]):

        @pl.when(index >= 0)
        def _(index=index, value=value):
            place = mirrored(index ^ here, coarse)
            sends[place] = sends[place] + value

    image_out[0] = image
    image_out[1] = spread + noise[0] * residual
    residual_out[...] = residual
    ratio_out[...] = in_lanes([alpha, norm_now, product], (fields, LANES))


def finish_kernel(sizes, me, received, shifted, images, residual, ratios, mine, solution_out, residual_out):
    fields, points, coarse, slots = sizes
    owner = (me[0] < coarse).astype(F32)
    spread = images[1] + shifted[0] + owner * received[0]
    scalars = received[1]
    alpha, norm_first, product_first = ratios[:, 0:1], ratios[:, 1:2], ratios[:, 2:3]
    inner, cross, norm_now = scalars[:, 0:1], scalars[:, 1:2], scalars[:, 2:3]
    beta = norm_now / norm_first
    product = inner + beta * (2.0 * cross + beta * product_first)
    step = norm_now / product
    observed = fields_of(mine[...], fields, points)
    direction = residual[...] + beta * observed
    solution_out[0] = alpha * observed + step * direction
    residual_out[0] = residual[...] - step * (spread + beta * images[0])


def call(kernel, sizes, outs, in_spaces, scratch=()):
    return pl.pallas_call(
        functools.partial(kernel, sizes),
        out_shape=[out if hasattr(out, "dtype") else jax.ShapeDtypeStruct(out, F32) for out in outs],
        in_specs=[pl.BlockSpec(memory_space=space) for space in in_spaces],
        out_specs=[pl.BlockSpec(memory_space=pltpu.VMEM)] * len(outs),
        scratch_shapes=list(scratch),
        compiler_params=pltpu.CompilerParams(vmem_limit_bytes=VMEM_LIMIT),
    )


def powers(size):
    assert size & (size - 1) == 0
    return [1 << bit for bit in range(size.bit_length() - 1)]


def swapped(value, axis, reach):
    return lax.ppermute(value, axis, [(at, at ^ reach) for at in range(lax.axis_size(axis))])


def exchanges():
    steps, bit = [], 0
    for axis in AXES[::-1]:
        for reach in powers(lax.axis_size(axis)):
            steps.append((axis, reach, bit))
            bit += 1
    return steps


def carry(shifted, ends, got, number, bit, down):
    full = (1 << bit) - 1
    low, upper = number & full, ((number >> bit) & 1) == 1
    takes = jnp.where(down, ~upper & (low == full), upper & (low == 0))
    return jnp.where(takes, got, shifted), jnp.where(upper ^ down, ends, got)


def local(locations, neighbours, observations, noise_prec):
    blocks, _, points = locations.shape
    fields = observations.shape[1]
    slots = neighbours.shape[1]
    assert blocks == 1
    coarse = lax.axis_size("dev")
    sizes = (fields, points, coarse, slots)
    depth = len(slot_list(slots)) * points
    pieces = points // LANES
    me = lax.axis_index(AXES).astype(jnp.int32)
    group = lax.axis_index("grp")
    smem, vmem = pltpu.SMEM, pltpu.VMEM
    square, tile = (points, points), (fields, points)
    steps = exchanges()

    lanes = [slice(at * LANES, (at + 1) * LANES) for at in range(pieces)]
    empty = jnp.zeros((1, LANES), F32)
    packed = [observations[0, :, cut] for cut in lanes]
    for cut in lanes:
        packed += [locations[0, :, cut], empty]
    mine = jnp.concatenate(packed, axis=0)
    noise = jnp.where(me < 0, 0.0, noise_prec)
    nbr = jnp.where(me < 0, -1, neighbours)
    before, table = mine[None], mine[None]
    for axis, reach, bit in steps[::-1]:
        got = swapped(jnp.concatenate([table, before], axis=0), axis, reach)
        low = (1 << bit) - 1
        before = jnp.where((me & low) == low, got[-1:], before)
        if axis == "grp":
            table = jnp.where((group & reach) != 0, got[:-1], table)
        else:
            table = jnp.concatenate([table, got[:-1]], axis=0)
    at = me.reshape(1)
    part, back, last = call(
        factor_kernel,
        sizes,
        [(coarse + 3,) + tile, (points, depth), square],
        [smem, smem] + [vmem] * 4,
        [pltpu.VMEM((slots, slots * points, points), F32)] * 2 + [pltpu.VMEM(square, F32)] * 2,
    )(nbr, at, before, table, mine, noise)

    half, odd = coarse // 2, (me & 1) == 1
    got = swapped(part[half:], "dev", 1)
    rows, scalars = part[:half] + got[:half], part[coarse : coarse + 1] + got[half : half + 1]
    up, down = got[half + 1 : half + 2], got[half + 2 :]
    near, ends, far = jnp.where(odd, up, down), jnp.where(odd, down, up), jnp.zeros_like(up)
    for axis, reach, bit in steps[1:]:
        got = swapped(jnp.concatenate([rows, scalars, ends], axis=0), axis, reach)
        rows, scalars = rows + got[:half], scalars + got[half : half + 1]
        far, ends = carry(far, ends, got[half + 1 :], me >> 1, bit - 1, odd)
    other_rows = swapped(rows, "dev", 1)
    sends, images, residual, ratios = call(
        step_kernel,
        sizes,
        [(coarse + 2,) + tile, (2,) + tile, tile, (fields, LANES)],
        [smem, smem] + [vmem] * 12,
    )(nbr, at, before, table, mine, noise, part, rows, other_rows, scalars, near, far, back, last)

    summed, ends, shifted = sends[:-1], sends[-1:], jnp.zeros_like(sends[-1:])
    for axis, reach, bit in steps:
        kept = (summed.shape[0] - 1) // 2 if axis == "dev" else 0
        got = swapped(jnp.concatenate([summed[kept:], ends], axis=0), axis, reach)
        if axis == "dev":
            summed = jnp.concatenate([summed[:kept], summed[-1:]], axis=0)
        summed = summed + got[:-1]
        shifted, ends = carry(shifted, ends, got[-1:], me, bit, True)
    return tuple(
        call(finish_kernel, sizes, [observations.shape] * 2, [smem] + [vmem] * 6)(
            at, summed, shifted, images, residual, ratios, mine
        )
    )


def solution(mesh):
    placed = (
        P(AXES, None, None),
        P(AXES, None),
        P(AXES, None, None),
        P(AXES, None, None),
    )
    return jax.shard_map(
        local,
        mesh=mesh,
        in_specs=placed,
        out_specs=(P(AXES, None, None), P(AXES, None, None)),
        check_vma=False,
    )
```

```python
import functools
import math

import jax
import jax.numpy as jnp
from jax import lax
from jax.experimental import pallas as pl
from jax.experimental.pallas import tpu as pltpu
from jax.sharding import PartitionSpec as P

SCALE_LENGTH = 0.5
NUGGET = 0.5
SQRT_THREE = math.sqrt(3.0)
LANES = 128
HIGHEST = lax.Precision.HIGHEST
F32 = jnp.float32
NN = (((1,), (0,)), ((), ()))
NT = (((1,), (1,)), ((), ()))
AXES = ("grp", "dev")
VMEM_LIMIT = 48 * 1024 * 1024
CLOSE = 2e-3
ROWS = 128
TOPS = (3, 4, 6)


def split(value):
    high = value.astype(jnp.bfloat16)
    return high, (value - high.astype(F32)).astype(jnp.bfloat16)


def dot(left, right, dims=NN, precision=None):
    return lax.dot_general(left, right, dims, precision=precision, preferred_element_type=F32)


def split_fine(value):
    high = value.astype(jnp.bfloat16)
    rest = value - high.astype(F32)
    middle = rest.astype(jnp.bfloat16)
    return high, middle, (rest - middle.astype(F32)).astype(jnp.bfloat16)


def taken(base, left, right, dims=NN, rows=None):
    count = len(left)
    pieces = []
    rows = rows or base.shape[0]
    for first in range(0, base.shape[0], rows):
        total = base[first : first + rows]
        cut = [part[first : first + rows] for part in left]
        for at in range(count):
            group = None
            for other in range(count - 1 - at, -1, -1):
                term = dot(cut[other], right[at], dims)
                group = term if group is None else group + term
            total = total - group
        pieces.append(total)
    return pieces[0] if len(pieces) == 1 else jnp.concatenate(pieces, axis=0)


def newton_levels(order):
    least = 1.0 - CLOSE
    levels = [(1.0, 1.0 / least - NUGGET)]
    while levels[-1][1] < order + NUGGET:
        reached = least / (2.0 - least)
        least = 1.0 - math.sqrt(1.0 - reached)
        levels.append((2.0 / (1.0 + reached), 1.0 / least - NUGGET))
    return levels


def inverse(matrix, ahead, guess, beside=()):
    order = matrix.shape[0]
    rows = lax.broadcasted_iota(jnp.int32, (order, order), 0)
    columns = lax.broadcasted_iota(jnp.int32, (order, order), 1)
    identity = (rows == columns).astype(F32)
    levels = newton_levels(order)
    last = len(levels) - 1
    tops = [top for top in TOPS if top < last] + [last]
    tops += [] if len(tops) > 1 else [last]
    bound = jnp.minimum(jnp.max(jnp.sum(jnp.abs(matrix), axis=0)), order + NUGGET)
    start = 2.0 / (NUGGET + levels[tops[0]][1])
    for below, top in zip(tops, tops[1:]):
        start = jnp.where(bound > levels[below][1], 2.0 / (NUGGET + levels[top][1]), start)
    ahead[...] = start * matrix
    guess[...] = start * identity

    def advance(scale, now, held, only_guess=False):
        now_parts = split(now)
        new_now = None if only_guess else scale * taken(2.0 * now, now_parts, now_parts, rows=ROWS)
        new_held = scale * taken(2.0 * held, split(held), now_parts, rows=ROWS)
        return new_now, new_held

    for below, top in list(zip(tops, tops[1:]))[::-1]:

        @pl.when(bound > levels[below][1])
        def _(below=below, top=top):
            for level in range(top, below, -1):
                ahead[...], guess[...] = advance(levels[level][0], ahead[...], guess[...])

    always = tops[0]
    beside = list(beside)

    def also(left):
        while len(beside) > left:
            beside.pop(0)()

    count = len(beside)
    for level in range(always, 1, -1):
        ahead[...], guess[...] = advance(levels[level][0], ahead[...], guess[...])
        also(count * level // (always + 1))
    guess[...] = advance(levels[1][0], ahead[...], guess[...], True)[1]
    also(count // (always + 1))
    held = guess[...]
    ahead[...] = -taken(identity, split_fine(matrix), split_fine(held), rows=ROWS)
    also(0)
    held = guess[...]
    guess[...] = taken(held, split(held), split(ahead[...]), rows=ROWS)
    return guess[...]


def slot_list(slots):
    return [slot for slot in range(slots) if slot != 1]


def mirrored(index, size):
    bits = size.bit_length() - 1
    return sum(((index >> bit) & 1) << (bits - 1 - bit) for bit in range(bits))


def covariance(first, second, alive, same):
    points = second.shape[1]
    rows_at_once = 64
    parts = []
    for start in range(0, points, rows_at_once):
        down = first[start : start + rows_at_once]
        total = None
        for k in range(3):
            offset = down[:, k : k + 1] - second[k : k + 1, :]
            total = offset * offset if total is None else total + offset * offset
        scaled = jnp.sqrt(total)
        value = (1.0 + scaled) * jnp.exp(-scaled) * alive
        if same:
            row = lax.broadcasted_iota(jnp.int32, value.shape, 0) + start
            column = lax.broadcasted_iota(jnp.int32, value.shape, 1)
            value = value + jnp.where(row == column, NUGGET * alive + (1.0 - alive), 0.0)
        parts.append(value)
    return jnp.concatenate(parts, axis=0)


def half_place(index, me, coarse):
    return index ^ ((me & 1) * (coarse // 2))


def live_of(index):
    return (index >= 0).astype(F32)


def fields_of(entry, fields, points):
    return jnp.concatenate([entry[at * fields : (at + 1) * fields] for at in range(points // LANES)], axis=1)


def places_of(entry, fields, points):
    pieces = points // LANES
    rows = [entry[fields * pieces + 4 * at :][:4] for at in range(pieces)]
    return jnp.concatenate(rows, axis=1) * (SQRT_THREE / SCALE_LENGTH)


def factor_kernel(
    sizes, nbr, me, before, table, mine, noise, part, back_high, back_low, last_high, last_low,
    columns, lower, ahead, guess,
):
    fields, points, coarse, slots = sizes
    used = slot_list(slots)
    own = len(used)
    ids = [nbr[0, slot] for slot in used] + [me[0]]
    here = lax.rem(me[0], coarse)
    entries = [before[0]]
    entries += [table[mirrored(jnp.maximum(index, 0) ^ here, coarse)] for index in ids[1:own]]
    entries += [mine[...]]
    live = [live_of(index) for index in ids]
    values = [fields_of(entry, fields, points) * alive for entry, alive in zip(entries, live)]
    places = [places_of(entry, fields, points) for entry in entries]
    turned = [jnp.transpose(jnp.concatenate([place, place], axis=0)) for place in places]

    def at(i, end=None):
        return pl.ds(i * points, ((i + 1 if end is None else end) - i) * points)

    def build(i, j):
        columns[j, at(i)] = covariance(turned[i], places[j], live[i] * live[j], i == j)

    build(0, 0)
    later = [functools.partial(build, i, j) for j in range(own + 1) for i in range(max(j, 1), own + 1)]
    for k in range(own):
        middle = inverse(columns[k, at(k)], ahead, guess, later if k == 0 else ())
        side = columns[k, at(k + 1, own + 1)]
        below = -taken(jnp.zeros_like(side), split_fine(side), split_fine(middle))
        lower[k, at(k + 1, own + 1)] = below
        side_parts, below_parts = split(side), split(below)
        for j in range(k + 1, own + 1):
            cut = (j - k - 1) * points
            left = [piece[cut:] for piece in below_parts]
            right = [piece[cut : cut + points] for piece in side_parts]
            columns[j, at(j, own + 1)] = taken(columns[j, at(j, own + 1)], left, right, NT)
    back = {}

    def go_back(k):
        total = lower[k, at(own)]
        for j in range(own - 1, k, -1):
            total = taken(total, back[j], split(lower[k, at(j)]))
        back[k] = split(total)
        place = slice(k * points, (k + 1) * points)
        back_high[:, place], back_low[:, place] = back[k]

    last = split(
        inverse(columns[own, at(own)], ahead, guess, [functools.partial(go_back, k) for k in range(own - 1, -1, -1)])
    )
    last_high[...], last_low[...] = last

    middle, spread, slot_parts = apply_block(values, back, last)
    own_part = spread + noise[0] * values[own]
    part[...] = jnp.zeros_like(part)
    product = jnp.sum(middle * spread + noise[0] * values[own] * values[own], axis=1, keepdims=True)
    square = jnp.sum(values[own] * values[own], axis=1, keepdims=True)
    part[coarse] = in_lanes([product, square], (fields, points))
    part[coarse + 1] = own_part
    part[coarse + 2] = slot_parts[0]
    for index, value in zip(ids, slot_parts + [own_part]):

        @pl.when((index >= 0) & (index < coarse))
        def _(index=index, value=value):
            place = half_place(index, me[0], coarse)
            part[place] = part[place] + value


def in_lanes(columns, shape):
    lane = lax.broadcasted_iota(jnp.int32, shape, 1)
    total = jnp.zeros(shape, F32)
    for at, column in enumerate(columns):
        total = jnp.where(lane == at, column, total)
    return total


def apply_block(values, back, last):
    own = len(values) - 1
    middle = values[own]
    for k in range(own):
        middle = taken(middle, split(values[k]), back[k], NT)
    spread = -taken(jnp.zeros_like(middle), split(middle), last)
    spread_parts = split(spread)
    slot_parts = [taken(jnp.zeros_like(middle), spread_parts, back[k]) for k in range(own)]
    return middle, spread, slot_parts


def step_kernel(
    sizes, nbr, me, before, table, mine, noise, part, rows, other_rows, scalars, near, far,
    back_high, back_low, last_high, last_low,
    sends, image_out, residual_out, ratio_out,
):
    fields, points, coarse, slots = sizes
    used = slot_list(slots)
    own = len(used)
    ids = [nbr[0, slot] for slot in used] + [me[0]]
    here = lax.rem(me[0], coarse)
    product = scalars[0, :, 0:1]
    norm_now = scalars[0, :, 1:2]
    alpha = norm_now / product
    half = coarse // 2
    even = (me[0] & 1) == 0
    values = []
    for at, index in enumerate(ids):
        place = half_place(jnp.clip(index, 0, coarse - 1), me[0], coarse)
        image = jnp.where(place < half, rows[place & (half - 1)], other_rows[place & (half - 1)])
        if at == 0:
            entry = before[0]
            image = jnp.where(index < coarse, image, jnp.where(even, far[0], near[0]) + part[coarse + 2])
        elif at == own:
            entry = mine[...]
            image = jnp.where(index < coarse, image, part[coarse + 1] + jnp.where(even, near[0], far[0]))
        else:
            entry = table[mirrored(jnp.maximum(index, 0) ^ here, coarse)]
        values.append((fields_of(entry, fields, points) - alpha * image) * live_of(index))
    places = [slice(k * points, (k + 1) * points) for k in range(own)]
    back = {k: (back_high[:, place], back_low[:, place]) for k, place in enumerate(places)}
    middle, spread, slot_parts = apply_block(values, back, (last_high[...], last_low[...]))
    residual = values[own]
    inner = jnp.sum(middle * spread + noise[0] * residual * residual, axis=1, keepdims=True)
    cross = jnp.sum(residual * image, axis=1, keepdims=True)
    square = jnp.sum(residual * residual, axis=1, keepdims=True)
    sends[...] = jnp.zeros_like(sends)
    sends[coarse] = in_lanes([inner, cross, square], (fields, points))
    sends[coarse + 1] = slot_parts[0]
    for index, value in zip(ids[1:own], slot_parts[1:]):

        @pl.when(index >= 0)
        def _(index=index, value=value):
            place = mirrored(index ^ here, coarse)
            sends[place] = sends[place] + value

    image_out[0] = image
    image_out[1] = spread + noise[0] * residual
    residual_out[...] = residual
    ratio_out[...] = in_lanes([alpha, norm_now, product], (fields, LANES))


def finish_kernel(sizes, me, received, shifted, images, residual, ratios, mine, solution_out, residual_out):
    fields, points, coarse, slots = sizes
    owner = (me[0] < coarse).astype(F32)
    spread = images[1] + shifted[0] + owner * received[0]
    scalars = received[1]
    alpha, norm_first, product_first = ratios[:, 0:1], ratios[:, 1:2], ratios[:, 2:3]
    inner, cross, norm_now = scalars[:, 0:1], scalars[:, 1:2], scalars[:, 2:3]
    beta = norm_now / norm_first
    product = inner + beta * (2.0 * cross + beta * product_first)
    step = norm_now / product
    observed = fields_of(mine[...], fields, points)
    direction = residual[...] + beta * observed
    solution_out[0] = alpha * observed + step * direction
    residual_out[0] = residual[...] - step * (spread + beta * images[0])


def call(kernel, sizes, outs, in_spaces, scratch=()):
    return pl.pallas_call(
        functools.partial(kernel, sizes),
        out_shape=[out if hasattr(out, "dtype") else jax.ShapeDtypeStruct(out, F32) for out in outs],
        in_specs=[pl.BlockSpec(memory_space=space) for space in in_spaces],
        out_specs=[pl.BlockSpec(memory_space=pltpu.VMEM)] * len(outs),
        scratch_shapes=list(scratch),
        compiler_params=pltpu.CompilerParams(vmem_limit_bytes=VMEM_LIMIT),
    )


def powers(size):
    assert size & (size - 1) == 0
    return [1 << bit for bit in range(size.bit_length() - 1)]


def swapped(value, axis, reach):
    return lax.ppermute(value, axis, [(at, at ^ reach) for at in range(lax.axis_size(axis))])


def exchanges():
    steps, bit = [], 0
    for axis in AXES[::-1]:
        for reach in powers(lax.axis_size(axis)):
            steps.append((axis, reach, bit))
            bit += 1
    return steps


def carry(shifted, ends, got, number, bit, down):
    full = (1 << bit) - 1
    low, upper = number & full, ((number >> bit) & 1) == 1
    takes = jnp.where(down, ~upper & (low == full), upper & (low == 0))
    return jnp.where(takes, got, shifted), jnp.where(upper ^ down, ends, got)


def local(locations, neighbours, observations, noise_prec):
    blocks, _, points = locations.shape
    fields = observations.shape[1]
    slots = neighbours.shape[1]
    assert blocks == 1
    coarse = lax.axis_size("dev")
    sizes = (fields, points, coarse, slots)
    depth = len(slot_list(slots)) * points
    pieces = points // LANES
    me = lax.axis_index(AXES).astype(jnp.int32)
    group = lax.axis_index("grp")
    smem, vmem = pltpu.SMEM, pltpu.VMEM
    square, tile = (points, points), (fields, points)
    steps = exchanges()

    lanes = [slice(at * LANES, (at + 1) * LANES) for at in range(pieces)]
    empty = jnp.zeros((1, LANES), F32)
    packed = [observations[0, :, cut] for cut in lanes]
    for cut in lanes:
        packed += [locations[0, :, cut], empty]
    mine = jnp.concatenate(packed, axis=0)
    noise = jnp.where(me < 0, 0.0, noise_prec)
    nbr = jnp.where(me < 0, -1, neighbours)
    before, table = mine[None], mine[None]
    for axis, reach, bit in steps[::-1]:
        got = swapped(jnp.concatenate([table, before], axis=0), axis, reach)
        low = (1 << bit) - 1
        before = jnp.where((me & low) == low, got[-1:], before)
        if axis == "grp":
            table = jnp.where((group & reach) != 0, got[:-1], table)
        else:
            table = jnp.concatenate([table, got[:-1]], axis=0)
    at = me.reshape(1)
    part, *inverses = call(
        factor_kernel,
        sizes,
        [(coarse + 3,) + tile] + [jax.ShapeDtypeStruct(shape, jnp.bfloat16) for shape in ((points, depth),) * 2 + (square,) * 2],
        [smem, smem] + [vmem] * 4,
        [pltpu.VMEM((slots, slots * points, points), F32)] * 2 + [pltpu.VMEM(square, F32)] * 2,
    )(nbr, at, before, table, mine, noise)

    half, odd = coarse // 2, (me & 1) == 1
    got = swapped(part[half:], "dev", 1)
    rows, scalars = part[:half] + got[:half], part[coarse : coarse + 1] + got[half : half + 1]
    up, down = got[half + 1 : half + 2], got[half + 2 :]
    near, ends, far = jnp.where(odd, up, down), jnp.where(odd, down, up), jnp.zeros_like(up)
    for axis, reach, bit in steps[1:]:
        got = swapped(jnp.concatenate([rows, scalars, ends], axis=0), axis, reach)
        rows, scalars = rows + got[:half], scalars + got[half : half + 1]
        far, ends = carry(far, ends, got[half + 1 :], me >> 1, bit - 1, odd)
    other_rows = swapped(rows, "dev", 1)
    sends, images, residual, ratios = call(
        step_kernel,
        sizes,
        [(coarse + 2,) + tile, (2,) + tile, tile, (fields, LANES)],
        [smem, smem] + [vmem] * 14,
    )(nbr, at, before, table, mine, noise, part, rows, other_rows, scalars, near, far, *inverses)

    summed, ends, shifted = sends[:-1], sends[-1:], jnp.zeros_like(sends[-1:])
    for axis, reach, bit in steps:
        kept = (summed.shape[0] - 1) // 2 if axis == "dev" else 0
        got = swapped(jnp.concatenate([summed[kept:], ends], axis=0), axis, reach)
        if axis == "dev":
            summed = jnp.concatenate([summed[:kept], summed[-1:]], axis=0)
        summed = summed + got[:-1]
        shifted, ends = carry(shifted, ends, got[-1:], me, bit, True)
    return tuple(
        call(finish_kernel, sizes, [observations.shape] * 2, [smem] + [vmem] * 6)(
            at, summed, shifted, images, residual, ratios, mine
        )
    )


def solution(mesh):
    placed = (
        P(AXES, None, None),
        P(AXES, None),
        P(AXES, None, None),
        P(AXES, None, None),
    )
    return jax.shard_map(
        local,
        mesh=mesh,
        in_specs=placed,
        out_specs=(P(AXES, None, None), P(AXES, None, None)),
        check_vma=False,
    )
```

```python
import functools
import math

import jax
import jax.numpy as jnp
from jax import lax
from jax.experimental import pallas as pl
from jax.experimental.pallas import tpu as pltpu
from jax.sharding import PartitionSpec as P

SCALE_LENGTH = 0.5
NUGGET = 0.5
SQRT_THREE = math.sqrt(3.0)
LANES = 128
HIGHEST = lax.Precision.HIGHEST
F32 = jnp.float32
NN = (((1,), (0,)), ((), ()))
NT = (((1,), (1,)), ((), ()))
AXES = ("grp", "dev")
VMEM_LIMIT = 48 * 1024 * 1024
CLOSE = 2e-3
ROWS = 128
TOPS = (3, 4, 6)


def split(value):
    high = value.astype(jnp.bfloat16)
    return high, (value - high.astype(F32)).astype(jnp.bfloat16)


def dot(left, right, dims=NN, precision=None):
    return lax.dot_general(left, right, dims, precision=precision, preferred_element_type=F32)


def split_fine(value):
    high = value.astype(jnp.bfloat16)
    rest = value - high.astype(F32)
    middle = rest.astype(jnp.bfloat16)
    return high, middle, (rest - middle.astype(F32)).astype(jnp.bfloat16)


def taken(base, left, right, dims=NN, rows=None):
    count = len(left)
    pieces = []
    rows = rows or base.shape[0]
    for first in range(0, base.shape[0], rows):
        total = base[first : first + rows]
        cut = [part[first : first + rows] for part in left]
        for at in range(count):
            group = None
            for other in range(count - 1 - at, -1, -1):
                term = dot(cut[other], right[at], dims)
                group = term if group is None else group + term
            total = total - group
        pieces.append(total)
    return pieces[0] if len(pieces) == 1 else jnp.concatenate(pieces, axis=0)


def newton_levels(order):
    least = 1.0 - CLOSE
    levels = [(1.0, 1.0 / least - NUGGET)]
    while levels[-1][1] < order + NUGGET:
        reached = least / (2.0 - least)
        least = 1.0 - math.sqrt(1.0 - reached)
        levels.append((2.0 / (1.0 + reached), 1.0 / least - NUGGET))
    return levels


def inverse(matrix, ahead, guess, beside=(), refine=True):
    order = matrix.shape[0]
    rows = lax.broadcasted_iota(jnp.int32, (order, order), 0)
    columns = lax.broadcasted_iota(jnp.int32, (order, order), 1)
    identity = (rows == columns).astype(F32)
    levels = newton_levels(order)
    last = len(levels) - 1
    tops = [top for top in TOPS if top < last] + [last]
    tops += [] if len(tops) > 1 else [last]
    bound = jnp.minimum(jnp.max(jnp.sum(jnp.abs(matrix), axis=0)), order + NUGGET)
    start = 2.0 / (NUGGET + levels[tops[0]][1])
    for below, top in zip(tops, tops[1:]):
        start = jnp.where(bound > levels[below][1], 2.0 / (NUGGET + levels[top][1]), start)
    ahead[...] = start * matrix
    guess[...] = start * identity

    def advance(scale, now, held, only_guess=False):
        now_parts = split(now)
        new_now = None if only_guess else scale * taken(2.0 * now, now_parts, now_parts, rows=ROWS)
        new_held = scale * taken(2.0 * held, split(held), now_parts, rows=ROWS)
        return new_now, new_held

    for below, top in list(zip(tops, tops[1:]))[::-1]:

        @pl.when(bound > levels[below][1])
        def _(below=below, top=top):
            for level in range(top, below, -1):
                ahead[...], guess[...] = advance(levels[level][0], ahead[...], guess[...])

    always = tops[0]
    beside = list(beside)

    def also(left):
        while len(beside) > left:
            beside.pop(0)()

    count = len(beside)
    for level in range(always, 1, -1):
        ahead[...], guess[...] = advance(levels[level][0], ahead[...], guess[...])
        also(count * level // (always + 1))
    guess[...] = advance(levels[1][0], ahead[...], guess[...], True)[1]
    also(count // (always + 1))
    if not refine:
        also(0)
        return guess[...]
    held = guess[...]
    ahead[...] = -taken(identity, split_fine(matrix), split_fine(held), rows=ROWS)
    also(0)
    held = guess[...]
    guess[...] = taken(held, split(held), split(ahead[...]), rows=ROWS)
    return guess[...]


def slot_list(slots):
    return [slot for slot in range(slots) if slot != 1]


def mirrored(index, size):
    bits = size.bit_length() - 1
    return sum(((index >> bit) & 1) << (bits - 1 - bit) for bit in range(bits))


def covariance(first, second, alive, same):
    points = second.shape[1]
    rows_at_once = 64
    parts = []
    for start in range(0, points, rows_at_once):
        down = first[start : start + rows_at_once]
        total = None
        for k in range(3):
            offset = down[:, k : k + 1] - second[k : k + 1, :]
            total = offset * offset if total is None else total + offset * offset
        scaled = jnp.sqrt(total)
        value = (1.0 + scaled) * jnp.exp(-scaled) * alive
        if same:
            row = lax.broadcasted_iota(jnp.int32, value.shape, 0) + start
            column = lax.broadcasted_iota(jnp.int32, value.shape, 1)
            value = value + jnp.where(row == column, NUGGET * alive + (1.0 - alive), 0.0)
        parts.append(value)
    return jnp.concatenate(parts, axis=0)


def half_place(index, me, coarse):
    return index ^ ((me & 1) * (coarse // 2))


def live_of(index):
    return (index >= 0).astype(F32)


def fields_of(entry, fields, points):
    return jnp.concatenate([entry[at * fields : (at + 1) * fields] for at in range(points // LANES)], axis=1)


def places_of(entry, fields, points):
    pieces = points // LANES
    rows = [entry[fields * pieces + 4 * at :][:4] for at in range(pieces)]
    return jnp.concatenate(rows, axis=1) * (SQRT_THREE / SCALE_LENGTH)


def factor_kernel(
    sizes, nbr, me, before, table, mine, noise, part, back_high, back_low, last_high, last_low,
    columns, lower, ahead, guess,
):
    fields, points, coarse, slots = sizes
    used = slot_list(slots)
    own = len(used)
    ids = [nbr[0, slot] for slot in used] + [me[0]]
    here = lax.rem(me[0], coarse)
    entries = [before[0]]
    entries += [table[mirrored(jnp.maximum(index, 0) ^ here, coarse)] for index in ids[1:own]]
    entries += [mine[...]]
    live = [live_of(index) for index in ids]
    values = [fields_of(entry, fields, points) * alive for entry, alive in zip(entries, live)]
    places = [places_of(entry, fields, points) for entry in entries]
    turned = [jnp.transpose(jnp.concatenate([place, place], axis=0)) for place in places]

    def at(i, end=None):
        return pl.ds(i * points, ((i + 1 if end is None else end) - i) * points)

    def build(i, j):
        columns[j, at(i)] = covariance(turned[i], places[j], live[i] * live[j], i == j)

    build(0, 0)
    later = [functools.partial(build, i, j) for j in range(own + 1) for i in range(max(j, 1), own + 1)]
    for k in range(own):
        middle = split(inverse(columns[k, at(k)], ahead, guess, later if k == 0 else (), refine=False))
        side = columns[k, at(k + 1, own + 1)]
        side_parts = split(side)
        rough = -taken(jnp.zeros_like(side), side_parts, middle)
        rest = taken(side, split_fine(rough), split_fine(columns[k, at(k)]))
        below = taken(rough, split(-rest), middle)
        lower[k, at(k + 1, own + 1)] = below
        below_parts = split(below)
        for j in range(k + 1, own + 1):
            cut = (j - k - 1) * points
            left = [piece[cut:] for piece in below_parts]
            right = [piece[cut : cut + points] for piece in side_parts]
            columns[j, at(j, own + 1)] = taken(columns[j, at(j, own + 1)], left, right, NT)
    back = {}

    def go_back(k):
        total = lower[k, at(own)]
        for j in range(own - 1, k, -1):
            total = taken(total, back[j], split(lower[k, at(j)]))
        back[k] = split(total)
        place = slice(k * points, (k + 1) * points)
        back_high[:, place], back_low[:, place] = back[k]

    last = split(
        inverse(columns[own, at(own)], ahead, guess, [functools.partial(go_back, k) for k in range(own - 1, -1, -1)])
    )
    last_high[...], last_low[...] = last

    middle, spread, slot_parts = apply_block(values, back, last)
    own_part = spread + noise[0] * values[own]
    part[...] = jnp.zeros_like(part)
    product = jnp.sum(middle * spread + noise[0] * values[own] * values[own], axis=1, keepdims=True)
    square = jnp.sum(values[own] * values[own], axis=1, keepdims=True)
    part[coarse] = in_lanes([product, square], (fields, points))
    part[coarse + 1] = own_part
    part[coarse + 2] = slot_parts[0]
    for index, value in zip(ids, slot_parts + [own_part]):

        @pl.when((index >= 0) & (index < coarse))
        def _(index=index, value=value):
            place = half_place(index, me[0], coarse)
            part[place] = part[place] + value


def in_lanes(columns, shape):
    lane = lax.broadcasted_iota(jnp.int32, shape, 1)
    total = jnp.zeros(shape, F32)
    for at, column in enumerate(columns):
        total = jnp.where(lane == at, column, total)
    return total


def apply_block(values, back, last):
    own = len(values) - 1
    middle = values[own]
    for k in range(own):
        middle = taken(middle, split(values[k]), back[k], NT)
    spread = -taken(jnp.zeros_like(middle), split(middle), last)
    spread_parts = split(spread)
    slot_parts = [taken(jnp.zeros_like(middle), spread_parts, back[k]) for k in range(own)]
    return middle, spread, slot_parts


def step_kernel(
    sizes, nbr, me, before, table, mine, noise, part, rows, other_rows, scalars, near, far,
    back_high, back_low, last_high, last_low,
    sends, image_out, residual_out, ratio_out,
):
    fields, points, coarse, slots = sizes
    used = slot_list(slots)
    own = len(used)
    ids = [nbr[0, slot] for slot in used] + [me[0]]
    here = lax.rem(me[0], coarse)
    product = scalars[0, :, 0:1]
    norm_now = scalars[0, :, 1:2]
    alpha = norm_now / product
    half = coarse // 2
    even = (me[0] & 1) == 0
    values = []
    for at, index in enumerate(ids):
        place = half_place(jnp.clip(index, 0, coarse - 1), me[0], coarse)
        image = jnp.where(place < half, rows[place & (half - 1)], other_rows[place & (half - 1)])
        if at == 0:
            entry = before[0]
            image = jnp.where(index < coarse, image, jnp.where(even, far[0], near[0]) + part[coarse + 2])
        elif at == own:
            entry = mine[...]
            image = jnp.where(index < coarse, image, part[coarse + 1] + jnp.where(even, near[0], far[0]))
        else:
            entry = table[mirrored(jnp.maximum(index, 0) ^ here, coarse)]
        values.append((fields_of(entry, fields, points) - alpha * image) * live_of(index))
    places = [slice(k * points, (k + 1) * points) for k in range(own)]
    back = {k: (back_high[:, place], back_low[:, place]) for k, place in enumerate(places)}
    middle, spread, slot_parts = apply_block(values, back, (last_high[...], last_low[...]))
    residual = values[own]
    inner = jnp.sum(middle * spread + noise[0] * residual * residual, axis=1, keepdims=True)
    cross = jnp.sum(residual * image, axis=1, keepdims=True)
    square = jnp.sum(residual * residual, axis=1, keepdims=True)
    sends[...] = jnp.zeros_like(sends)
    sends[coarse] = in_lanes([inner, cross, square], (fields, points))
    sends[coarse + 1] = slot_parts[0]
    for index, value in zip(ids[1:own], slot_parts[1:]):

        @pl.when(index >= 0)
        def _(index=index, value=value):
            place = mirrored(index ^ here, coarse)
            sends[place] = sends[place] + value

    image_out[0] = image
    image_out[1] = spread + noise[0] * residual
    residual_out[...] = residual
    ratio_out[...] = in_lanes([alpha, norm_now, product], (fields, LANES))


def finish_kernel(sizes, me, received, shifted, images, residual, ratios, mine, solution_out, residual_out):
    fields, points, coarse, slots = sizes
    owner = (me[0] < coarse).astype(F32)
    spread = images[1] + shifted[0] + owner * received[0]
    scalars = received[1]
    alpha, norm_first, product_first = ratios[:, 0:1], ratios[:, 1:2], ratios[:, 2:3]
    inner, cross, norm_now = scalars[:, 0:1], scalars[:, 1:2], scalars[:, 2:3]
    beta = norm_now / norm_first
    product = inner + beta * (2.0 * cross + beta * product_first)
    step = norm_now / product
    observed = fields_of(mine[...], fields, points)
    direction = residual[...] + beta * observed
    solution_out[0] = alpha * observed + step * direction
    residual_out[0] = residual[...] - step * (spread + beta * images[0])


def call(kernel, sizes, outs, in_spaces, scratch=()):
    return pl.pallas_call(
        functools.partial(kernel, sizes),
        out_shape=[out if hasattr(out, "dtype") else jax.ShapeDtypeStruct(out, F32) for out in outs],
        in_specs=[pl.BlockSpec(memory_space=space) for space in in_spaces],
        out_specs=[pl.BlockSpec(memory_space=pltpu.VMEM)] * len(outs),
        scratch_shapes=list(scratch),
        compiler_params=pltpu.CompilerParams(vmem_limit_bytes=VMEM_LIMIT),
    )


def powers(size):
    assert size & (size - 1) == 0
    return [1 << bit for bit in range(size.bit_length() - 1)]


def swapped(value, axis, reach):
    return lax.ppermute(value, axis, [(at, at ^ reach) for at in range(lax.axis_size(axis))])


def exchanges():
    steps, bit = [], 0
    for axis in AXES[::-1]:
        for reach in powers(lax.axis_size(axis)):
            steps.append((axis, reach, bit))
            bit += 1
    return steps


def carry(shifted, ends, got, number, bit, down):
    full = (1 << bit) - 1
    low, upper = number & full, ((number >> bit) & 1) == 1
    takes = jnp.where(down, ~upper & (low == full), upper & (low == 0))
    return jnp.where(takes, got, shifted), jnp.where(upper ^ down, ends, got)


def local(locations, neighbours, observations, noise_prec):
    blocks, _, points = locations.shape
    fields = observations.shape[1]
    slots = neighbours.shape[1]
    assert blocks == 1
    coarse = lax.axis_size("dev")
    sizes = (fields, points, coarse, slots)
    depth = len(slot_list(slots)) * points
    pieces = points // LANES
    me = lax.axis_index(AXES).astype(jnp.int32)
    group = lax.axis_index("grp")
    smem, vmem = pltpu.SMEM, pltpu.VMEM
    square, tile = (points, points), (fields, points)
    steps = exchanges()

    lanes = [slice(at * LANES, (at + 1) * LANES) for at in range(pieces)]
    empty = jnp.zeros((1, LANES), F32)
    packed = [observations[0, :, cut] for cut in lanes]
    for cut in lanes:
        packed += [locations[0, :, cut], empty]
    mine = jnp.concatenate(packed, axis=0)
    noise = jnp.where(me < 0, 0.0, noise_prec)
    nbr = jnp.where(me < 0, -1, neighbours)
    before, table = mine[None], mine[None]
    for axis, reach, bit in steps[::-1]:
        got = swapped(jnp.concatenate([table, before], axis=0), axis, reach)
        low = (1 << bit) - 1
        before = jnp.where((me & low) == low, got[-1:], before)
        if axis == "grp":
            table = jnp.where((group & reach) != 0, got[:-1], table)
        else:
            table = jnp.concatenate([table, got[:-1]], axis=0)
    at = me.reshape(1)
    part, *inverses = call(
        factor_kernel,
        sizes,
        [(coarse + 3,) + tile] + [jax.ShapeDtypeStruct(shape, jnp.bfloat16) for shape in ((points, depth),) * 2 + (square,) * 2],
        [smem, smem] + [vmem] * 4,
        [pltpu.VMEM((slots, slots * points, points), F32)] * 2 + [pltpu.VMEM(square, F32)] * 2,
    )(nbr, at, before, table, mine, noise)

    half, odd = coarse // 2, (me & 1) == 1
    got = swapped(part[half:], "dev", 1)
    rows, scalars = part[:half] + got[:half], part[coarse : coarse + 1] + got[half : half + 1]
    up, down = got[half + 1 : half + 2], got[half + 2 :]
    near, ends, far = jnp.where(odd, up, down), jnp.where(odd, down, up), jnp.zeros_like(up)
    for axis, reach, bit in steps[1:]:
        got = swapped(jnp.concatenate([rows, scalars, ends], axis=0), axis, reach)
        rows, scalars = rows + got[:half], scalars + got[half : half + 1]
        far, ends = carry(far, ends, got[half + 1 :], me >> 1, bit - 1, odd)
    other_rows = swapped(rows, "dev", 1)
    sends, images, residual, ratios = call(
        step_kernel,
        sizes,
        [(coarse + 2,) + tile, (2,) + tile, tile, (fields, LANES)],
        [smem, smem] + [vmem] * 14,
    )(nbr, at, before, table, mine, noise, part, rows, other_rows, scalars, near, far, *inverses)

    summed, ends, shifted = sends[:-1], sends[-1:], jnp.zeros_like(sends[-1:])
    for axis, reach, bit in steps:
        kept = (summed.shape[0] - 1) // 2 if axis == "dev" else 0
        got = swapped(jnp.concatenate([summed[kept:], ends], axis=0), axis, reach)
        if axis == "dev":
            summed = jnp.concatenate([summed[:kept], summed[-1:]], axis=0)
        summed = summed + got[:-1]
        shifted, ends = carry(shifted, ends, got[-1:], me, bit, True)
    return tuple(
        call(finish_kernel, sizes, [observations.shape] * 2, [smem] + [vmem] * 6)(
            at, summed, shifted, images, residual, ratios, mine
        )
    )


def solution(mesh):
    placed = (
        P(AXES, None, None),
        P(AXES, None),
        P(AXES, None, None),
        P(AXES, None, None),
    )
    return jax.shard_map(
        local,
        mesh=mesh,
        in_specs=placed,
        out_specs=(P(AXES, None, None), P(AXES, None, None)),
        check_vma=False,
    )
```
